32 devices in a mesh: vol: 4 (over y, core), zs: 8 (over z, x).
Axes of the slice: x: 2, y: 2, z: 4, core: 2. Of those that a mesh axis runs over, the one named last changes fastest.
Arguments:
- volume: bfloat16 [8, 128, 256], P('zs', 'vol'), may hold values from -6 to 6
- first_weight: bfloat16 [9, 12], replicated, may hold values from -3 to 3
- first_offset: float32 [12], replicated, may hold values from -2 to 2
- second_weight: bfloat16 [9, 12, 12], replicated, may hold values from -0.875 to 0.875
- second_offset: float32 [12], replicated, may hold values from -2 to 2
- reduce_conv_weight: bfloat16 [4, 12, 24], replicated, may hold values from -1.25 to 1.25
- reduce_conv_bias: float32 [24], replicated, may hold values from -2 to 2
- deep_weight: bfloat16 [27, 24, 24], replicated, may hold values from -0.3125 to 0.3125
- deep_offset: float32 [24], replicated, may hold values from -2 to 2
Outputs:
- affinity: bfloat16 [8, 24, 64, 128], P(None, None, ('vol', 'zs'))
The draws below stay inside these ranges and needn't reach their ends.
All inputs are finite; a program needn't handle non-finite values.
Results may differ from the reference program's by a relative error of at most 0.0065.
Values may be sent and summed in bfloat16 or wider, within the bound.
No kernel may reach another device: no remote copies, remote signals or barrier semaphores. Data moves between devices by JAX's collectives and lax.ppermute only.
A program may use at most 192 MiB of HBM per device.

```python
import jax
import jax.numpy as jnp
from jax import lax

CH_PLANE = 12
CH_DEEP = 24
PY = 256
X = 128
Z = 8


def block_levels(rng, dims, shards, smallest, top_value):
    level = 1.0
    for position, parts in shards:
        heights = jax.random.uniform(jax.random.fold_in(jax.random.fold_in(rng, 6), position), (parts,), jnp.float32, smallest / len(shards), top_value / len(shards))
        level = level * jnp.repeat(jnp.exp(heights), dims[position] // parts).reshape((-1,) + (1,) * (len(dims) - 1 - position))
    return level


def normal_values(rng, dims, width, limit, split=(), kind=jnp.bfloat16):
    loudness = block_levels(rng, dims, split, -0.22, 0.18) if split else 1.0
    array = jax.random.normal(rng, dims, jnp.float32) * width * loudness
    return jnp.minimum(jnp.maximum(array, -limit), limit).astype(kind)


def setup_inputs(seed: int = 0) -> dict:
    streams_of = jax.random.split(jax.random.key(seed), 10)
    volume = normal_values(streams_of[0], (Z, X, PY), 1.0, 6.0, ((0, 8), (1, 4)))
    first_weight = normal_values(streams_of[1], (9, CH_PLANE), 4 ** -0.5, 3.0)
    first_offset = normal_values(streams_of[2], (CH_PLANE,), 0.5, 2.0, (), jnp.float32)
    second_weight = normal_values(streams_of[3], (9, CH_PLANE, CH_PLANE), 54 ** -0.5, 0.875)
    second_offset = normal_values(streams_of[4], (CH_PLANE,), 0.5, 2.0, (), jnp.float32)
    reduce_conv_weight = normal_values(streams_of[5], (4, CH_PLANE, CH_DEEP), 24 ** -0.5, 1.25)
    reduce_conv_bias = normal_values(streams_of[6], (CH_DEEP,), 0.5, 2.0, (), jnp.float32)
    deep_weight = normal_values(streams_of[7], (27, CH_DEEP, CH_DEEP), 324 ** -0.5, 0.3125)
    deep_offset = normal_values(streams_of[8], (CH_DEEP,), 0.5, 2.0, (), jnp.float32)
    return dict(volume=volume, first_weight=first_weight, first_offset=first_offset, second_weight=second_weight, second_offset=second_offset, reduce_conv_weight=reduce_conv_weight, reduce_conv_bias=reduce_conv_bias, deep_weight=deep_weight, deep_offset=deep_offset)


def plane_conv(field, weight, offset):
    padded = jnp.pad(field, ((0, 0), (1, 1), (1, 1)))
    row_count = field.shape[1]
    col_count = field.shape[2]
    summed = jnp.zeros((weight.shape[2], row_count, col_count), jnp.float32)
    for along_x in range(3):
        for along_y in range(3):
            window = padded[:, along_x:along_x + row_count, along_y:along_y + col_count]
            summed = summed + jnp.einsum("cxy,cd->dxy", window, weight[3 * along_x + along_y])
    return summed + offset[:, None, None]


def reference(volume, first_weight, first_offset, second_weight, second_offset, reduce_conv_weight, reduce_conv_bias, deep_weight, deep_offset):
    plane_chan = first_weight.shape[1]
    deep_chan = reduce_conv_weight.shape[2]
    first_kernel = first_weight.astype(jnp.float32).reshape(9, 1, plane_chan)
    latter_conv_kernel = second_weight.astype(jnp.float32)
    down_kernel = reduce_conv_weight.astype(jnp.float32).reshape(2, 2, plane_chan, deep_chan)
    deep_kernel = deep_weight.astype(jnp.float32)

    def slice_section(plane):
        field = plane.astype(jnp.float32)[None]
        first = jax.nn.relu(plane_conv(field, first_kernel, first_offset)).astype(jnp.bfloat16)
        latter_conv = jax.nn.relu(plane_conv(first.astype(jnp.float32), latter_conv_kernel, second_offset)).astype(jnp.bfloat16)
        half_x = latter_conv.shape[1] // 2
        half_y = latter_conv.shape[2] // 2
        blocks = latter_conv.astype(jnp.float32).reshape(plane_chan, half_x, 2, half_y, 2)
        summed = jnp.einsum("cxayb,abcd->dxy", blocks, down_kernel) + reduce_conv_bias[:, None, None]
        return jax.nn.relu(summed).astype(jnp.bfloat16)

    coarse = lax.map(slice_section, volume)
    padded_depth = jnp.pad(coarse, ((1, 1), (0, 0), (0, 0), (0, 0)))
    row_count = coarse.shape[2]
    col_count = coarse.shape[3]

    def deep_slice(depth_index):
        window = lax.dynamic_slice_in_dim(padded_depth, depth_index, 3, 0).astype(jnp.float32)
        window = jnp.pad(window, ((0, 0), (0, 0), (1, 1), (1, 1)))
        summed = jnp.zeros((deep_chan, row_count, col_count), jnp.float32)
        for along_z in range(3):
            for along_x in range(3):
                for along_y in range(3):
                    piece = window[along_z, :, along_x:along_x + row_count, along_y:along_y + col_count]
                    summed = summed + jnp.einsum("cxy,cd->dxy", piece, deep_kernel[9 * along_z + 3 * along_x + along_y])
        return jax.nn.relu(summed + deep_offset[:, None, None]).astype(jnp.bfloat16)

    return lax.map(deep_slice, jnp.arange(coarse.shape[0], dtype=jnp.int32))
```

```python
import functools

import jax
import jax.numpy as jnp
from jax import lax
from jax.experimental import pallas as pl
from jax.experimental.pallas import tpu as pltpu
from jax.sharding import PartitionSpec as P

TILE = 16
SHIFTS = ((1, 2, 0, None), (0, 1, None, 2))
F32 = jnp.float32
BF16 = jnp.bfloat16


def iota(shape, dim):
    return lax.broadcasted_iota(jnp.int32, shape, dim)


def ceil_to(value, step):
    return -(-value // step) * step


def div(value, by):
    if by & (by - 1) == 0:
        return lax.shift_right_logical(value, by.bit_length() - 1)
    return lax.shift_right_logical(value * (-(-65536 // by)), 16)


def one_hot(condition):
    return jnp.where(condition, 1.0, 0.0).astype(BF16)


def nt_dot(lhs, rhs):
    return lax.dot_general(lhs, rhs, (((1,), (1,)), ((), ())), preferred_element_type=F32)


def nn_dot(lhs, rhs):
    return jnp.dot(lhs, rhs, preferred_element_type=F32)


class Sizes:
    def __init__(self, volume, first_weight, reduce_conv_weight, vols, members):
        self.depth = volume.shape[0] * members
        self.cols = volume.shape[2]
        self.half = self.cols // 2
        self.fine_rows = volume.shape[1] * vols
        self.rows = volume.shape[1]
        self.strip = volume.shape[1] // 2 // members
        self.chan = first_weight.shape[1]
        self.deep = reduce_conv_weight.shape[2]
        self.coarse_rows = self.strip + 2
        self.second_rows = 2 * self.coarse_rows
        self.first_rows = self.second_rows + 2
        self.window = self.first_rows + 2
        self.pieces = self.window // 4
        self.lines = ceil_to(self.window, TILE)
        self.ones1 = self.first_rows * self.chan
        self.m1 = ceil_to(self.ones1 + 3, TILE)
        self.m2 = self.second_rows * self.chan
        self.m3 = self.coarse_rows * self.deep
        self.m4 = self.strip * self.deep

    def base(self, member):
        return 2 * self.strip * member - 4


def sort_kernel(z, own_ref, sort_ref, sorted_ref):
    core = lax.rem(lax.axis_index("vol"), 2)
    shape = (z.cols, z.half)
    sort = one_hot(iota(shape, 0) == 2 * iota(shape, 1) + core)
    sort_ref[...] = sort
    for s in range(own_ref.shape[0]):
        sorted_ref[s] = nn_dot(own_ref[s], sort)


def pack_kernel(z, chips, members, own_ref, sort_ref, other_ref, packed_ref):
    vol = lax.axis_index("vol")
    chip = lax.div(vol, 2)
    first_core = vol - 2 * chip == 0
    packed_ref[...] = jnp.zeros(packed_ref.shape, BF16)
    slices = own_ref.shape[0]
    empty = jnp.zeros((4, z.half), BF16)
    for s in range(slices):
        own, other = own_ref[s], nn_dot(other_ref[s], sort_ref[...])
        lines = stacked([jnp.where(first_core, own, other), jnp.where(first_core, other, own)])
        pieces = [lines[row : row + 4].astype(BF16) for row in range(0, 2 * z.rows, 4)]

        def put(to, first):
            for piece in range(z.pieces):
                at = first // 4 + piece
                value = pieces[at] if 0 <= at < len(pieces) else empty
                packed_ref[(to * slices + s) * z.pieces + piece] = value

        for core in range(2):
            for member in range(members):
                put((2 * chip + core) * members + member, core * z.rows + z.base(member))

        @pl.when(chip < chips - 1)
        def _():
            put(2 * (chip + 1) * members, 2 * z.rows - 4)

        @pl.when(chip > 0)
        def _():
            put(2 * chip * members - 1, 4 - z.window)


def prepare_kernel(
    z, members, w1_ref, b1_ref, w2_ref, b2_ref, w3_ref, b3_ref, w4_ref, b4_ref,
    k1_ref, k2_ref, k3_ref, k4_ref,
):
    member = lax.axis_index("zs")
    start = (lax.axis_index("vol") * members + member) * (2 * z.strip)
    def spread(rows, offsets, period, stretch):
        row = div(iota((rows, period), 0), stretch)
        at = row - div(row, period) * period
        picked = jnp.where(at == iota((rows, period), 1), offsets, 0.0)
        return jnp.sum(picked, axis=1, keepdims=True)

    def bias_terms(column, at):
        high = column.astype(BF16).astype(F32)
        middle = (column - high).astype(BF16).astype(F32)
        low = column - high - middle
        return jnp.where(at == 0, high, jnp.where(at == 1, middle, jnp.where(at == 2, low, 0.0)))

    row = iota((z.m1, z.chan), 0)
    pick = one_hot(row - div(row, z.chan) * z.chan == iota((z.m1, z.chan), 1))
    taps = nt_dot(pick, w1_ref[...]).astype(BF16)
    shape = (z.m1, 4 * z.lines)
    x = div(iota(shape, 0), z.chan)
    col = iota(shape, 1)
    line = col - div(col, z.lines) * z.lines
    inside = (start - 3 + x >= 0) & (start - 3 + x < z.fine_rows) & (x < z.first_rows)
    block = div(iota((9, 4 * z.lines), 1), z.lines)
    narrow = (z.m1, TILE)
    row, col = iota(narrow, 0), iota(narrow, 1)
    narrow_x = div(row, z.chan)
    narrow_inside = (start - 3 + narrow_x >= 0) & (start - 3 + narrow_x < z.fine_rows)
    bias = jnp.where(narrow_inside, bias_terms(spread(z.m1, b1_ref[...], z.chan, 1), col), 0.0)
    ones = jnp.where((row < z.ones1 + 3) & (col == 0), 1.0, 0.0)
    bias = jnp.where(row < z.ones1, bias, ones).astype(BF16)
    for parity, shifts in enumerate(SHIFTS):
        shift = jnp.full(block.shape, 9, jnp.int32)
        for number, value in enumerate(shifts):
            if value is not None:
                shift = jnp.where(block == number, value, shift)
        total = jnp.zeros(shape, F32)
        for i in range(3):
            level = nn_dot(taps, one_hot(iota(block.shape, 0) == 3 * i + shift))
            total += jnp.where(inside & (line == x + i), level, 0.0)
        k1_ref[parity * z.m1 : (parity + 1) * z.m1, : 4 * z.lines] = total.astype(BF16)
        k1_ref[parity * z.m1 : (parity + 1) * z.m1, 4 * z.lines :] = bias

    row = iota((z.m2, z.chan), 0)
    pick = one_hot(row - div(row, z.chan) * z.chan == iota((z.m2, z.chan), 1))
    col = iota((z.chan, z.m1), 1)
    widen = one_hot(col - div(col, z.chan) * z.chan == iota((z.chan, z.m1), 0))
    shape = (z.m2, z.m1)
    lag = div(iota(shape, 1), z.chan) - div(iota(shape, 0), z.chan)
    bias = bias_terms(spread(z.m2, b2_ref[...], z.chan, 1), iota(shape, 1) - z.ones1)
    for s in range(3):
        total = bias if s == 1 else jnp.zeros(shape, F32)
        for i in range(3):
            level = nn_dot(nt_dot(pick, w2_ref[3 * i + s]).astype(BF16), widen)
            total += jnp.where(lag == i, level, 0.0)
        total = total.astype(BF16)
        for parity, shifts in enumerate(SHIFTS):
            at = shifts.index(s)
            k2_ref[parity * z.m2 : (parity + 1) * z.m2, at * z.m1 : (at + 1) * z.m1] = total
    for parity, shifts in enumerate(SHIFTS):
        at = shifts.index(None)
        k2_ref[parity * z.m2 : (parity + 1) * z.m2, at * z.m1 : (at + 1) * z.m1] = jnp.zeros(shape, BF16)

    row = iota((z.m3, z.deep), 0)
    u = div(row, z.deep)
    pick = one_hot(row - u * z.deep == iota((z.m3, z.deep), 1))
    col = iota((z.chan, z.m2), 1)
    widen = one_hot(col - div(col, z.chan) * z.chan == iota((z.chan, z.m2), 0))
    shape = (z.m3, z.m2)
    u = div(iota(shape, 0), z.deep)
    lag = div(iota(shape, 1), z.chan) - 2 * u
    inside = (start + 2 * u >= 2) & (start + 2 * u < z.fine_rows + 2)
    for b in range(2):
        total = jnp.zeros(shape, F32)
        for a in range(2):
            level = nn_dot(nt_dot(pick, w3_ref[2 * a + b]).astype(BF16), widen)
            total += jnp.where(inside & (lag == a), level, 0.0)
        k3_ref[:, b * z.m2 : (b + 1) * z.m2] = total.astype(BF16)
    shape = (z.m3, TILE)
    u = div(iota(shape, 0), z.deep)
    inside = (start + 2 * u >= 2) & (start + 2 * u < z.fine_rows + 2)
    bias = bias_terms(spread(z.m3, b3_ref[...], z.deep, 1), iota(shape, 1))
    k3_ref[:, 2 * z.m2 :] = jnp.where(inside, bias, 0.0).astype(BF16)

    row = iota((z.m4, z.deep), 0)
    pick = one_hot(div(row, z.strip) == iota((z.m4, z.deep), 1))
    col = iota((z.deep, z.m3), 1)
    widen = one_hot(col - div(col, z.deep) * z.deep == iota((z.deep, z.m3), 0))
    shape = (z.m4, z.m3)
    row = iota(shape, 0)
    lag = div(iota(shape, 1), z.deep) - (row - div(row, z.strip) * z.strip)
    for i in range(3):
        for s in range(3):
            total = jnp.zeros(shape, F32)
            for j in range(3):
                level = nn_dot(nt_dot(pick, w4_ref[9 * i + 3 * j + s]).astype(BF16), widen)
                total += jnp.where(lag == j, level, 0.0)
            k4_ref[i * z.m4 : (i + 1) * z.m4, s * z.m3 : (s + 1) * z.m3] = total.astype(BF16)
    shape = (z.m4, TILE)
    bias = bias_terms(spread(z.m4, b4_ref[...], z.deep, z.strip), iota(shape, 1))
    for i in range(3):
        terms = bias if i == 1 else jnp.zeros(shape, F32)
        k4_ref[i * z.m4 : (i + 1) * z.m4, 3 * z.m3 :] = terms.astype(BF16)


def relu(value):
    return jnp.maximum(value.astype(BF16), 0)


def side_by_side(values):
    return jnp.concatenate(values, axis=1)


def stacked(values):
    return jnp.concatenate(values, axis=0)


def moved(value, by, lanes):
    width = value.shape[1]
    turned = pltpu.roll(value, by % width, axis=1)
    edge = 0 if by == 1 else width - 1
    return jnp.where(lanes == edge, jnp.zeros_like(turned), turned)


def main_kernel(
    z, chips, got_ref, k1_ref, k2_ref, k3_ref, k4_ref, out_ref, coarse,
):
    chip = lax.div(lax.axis_index("vol"), 2)
    sources = [chip]
    if chips > 1:
        sources.append(lax.rem(chip + 1, chips))
    if chips > 2:
        sources.append(lax.rem(chip + chips - 1, chips))
    group = min(z.depth, 8)
    groups = z.depth // group
    n = z.half
    ones = jnp.ones((TILE, group * n), BF16)
    blanks = [jnp.zeros((z.lines - z.window, n), F32)] if z.lines > z.window else []
    lanes0 = iota((z.lines, n), 1)
    lanes1 = iota((z.m1, n), 1)
    lanes3 = iota((z.m3, n), 1)
    if groups > 1:
        coarse[0] = jnp.zeros((z.m3, n), BF16)
        coarse[z.depth + 1] = jnp.zeros((z.m3, n), BF16)

    def blocks(evens, odds, lanes):
        odds_right = [moved(odd, 1, lanes) for odd in odds]
        evens_left = [moved(even, -1, lanes) for even in evens]
        return [side_by_side(pair) for pair in (evens, odds, odds_right, evens_left)]

    def lines_of(k, core):
        pieces = []
        for piece in range(z.pieces):
            at = k * z.pieces + piece
            pieces.append(sum(got_ref[source, core, at].astype(F32) for source in sources))
        return stacked(pieces + blanks)

    def split(value):
        return [value[:, k : k + n] for k in range(0, value.shape[1], n)]

    def leading(base):
        evens, odds = ([lines_of(base + k, core) for k in range(group)] for core in range(2))
        field = stacked([stacked(blocks(evens, odds, lanes0)).astype(BF16), ones])
        first = relu(nn_dot(k1_ref[...], field))
        moves = blocks(split(first[: z.m1]), split(first[z.m1 :]), lanes1)[2:]
        second = relu(nn_dot(k2_ref[...], stacked([first] + moves)))
        reduced = relu(nn_dot(k3_ref[...], stacked([second, ones])))
        for k, plane in enumerate(split(reduced)):
            coarse[base + k + 1] = plane

    def trailing(base):
        around = list(range(-1, group + 1)) if groups > 1 else list(range(group))
        planes = [coarse[base + k + 1] for k in around]
        field = stacked([
            side_by_side([moved(plane, 1, lanes3) for plane in planes]),
            side_by_side(planes),
            side_by_side([moved(plane, -1, lanes3) for plane in planes]),
            jnp.ones((TILE, len(planes) * n), BF16),
        ])
        terms = split(nn_dot(k4_ref[...], field))
        for k in range(group):
            parts = [
                terms[around.index(k + i - 1)][i * z.m4 : (i + 1) * z.m4] for i in range(3) if k + i - 1 in around
            ]
            out_ref[base + k] = relu(sum(parts[1:], parts[0]))

    if groups == 1:
        leading(0)
        trailing(0)
    else:
        pl.loop(0, groups)(lambda g: leading(g * group))
        pl.loop(0, groups)(lambda g: trailing(g * group))


def shards(
    volume, first_weight, first_offset, second_weight, second_offset,
    reduce_conv_weight, reduce_conv_bias, deep_weight, deep_offset,
):
    vols, members = lax.axis_size("vol"), lax.axis_size("zs")
    z = Sizes(volume, first_weight, reduce_conv_weight, vols, members)
    slices = volume.shape[0]
    vmem = pl.BlockSpec(memory_space=pltpu.VMEM)
    like = jax.ShapeDtypeStruct
    chips = vols // 2
    other = lax.ppermute(volume, "vol", [(v, v ^ 1) for v in range(vols)])
    sort, own = pl.pallas_call(
        functools.partial(sort_kernel, z),
        out_shape=(like((z.cols, z.half), BF16), like((slices, z.rows, z.half), F32)),
        in_specs=[vmem],
        out_specs=(vmem,) * 2,
        compiler_params=pltpu.CompilerParams(vmem_limit_bytes=16 * 1024 * 1024),
        cost_estimate=pl.CostEstimate(flops=5_000_000, bytes_accessed=100_000, transcendentals=0),
        name="sort",
    )(volume)
    packed = pl.pallas_call(
        functools.partial(pack_kernel, z, chips, members),
        out_shape=like((vols * members * slices * z.pieces, 4, z.half), BF16),
        in_specs=[vmem] * 3,
        out_specs=vmem,
        compiler_params=pltpu.CompilerParams(vmem_limit_bytes=16 * 1024 * 1024),
        name="pack",
    )(own, sort, other)
    packed, *parameters = lax.optimization_barrier((
        packed, first_weight, first_offset, second_weight, second_offset,
        reduce_conv_weight, reduce_conv_bias, deep_weight, deep_offset,
    ))
    got = lax.all_to_all(packed, ("vol", "zs"), split_axis=0, concat_axis=0, tiled=True)
    got = got.reshape(chips, 2, z.depth * z.pieces, 4, z.half)
    prepared = pl.pallas_call(
        functools.partial(prepare_kernel, z, members),
        out_shape=(
            like((2 * z.m1, 4 * z.lines + TILE), BF16),
            like((2 * z.m2, 4 * z.m1), BF16),
            like((z.m3, 2 * z.m2 + TILE), BF16),
            like((3 * z.m4, 3 * z.m3 + TILE), BF16),
        ),
        in_specs=[vmem] * 8,
        out_specs=(vmem,) * 4,
        compiler_params=pltpu.CompilerParams(vmem_limit_bytes=16 * 1024 * 1024),
        cost_estimate=pl.CostEstimate(flops=50_000_000, bytes_accessed=1_000_000, transcendentals=0),
        name="prepare",
    )(
        *(value[None] if value.ndim == 1 else value for value in parameters)
    )
    affinity = pl.pallas_call(
        functools.partial(main_kernel, z, chips),
        out_shape=like((z.depth, z.m4, z.half), BF16),
        in_specs=[vmem] * 5,
        out_specs=vmem,
        scratch_shapes=[
            pltpu.VMEM((z.depth + 2, z.m3, z.half), BF16),
        ],
        compiler_params=pltpu.CompilerParams(vmem_limit_bytes=32 * 1024 * 1024),
        cost_estimate=pl.CostEstimate(flops=2_000_000_000, bytes_accessed=2_000_000, transcendentals=0),
        name="encode",
    )(got, *prepared)
    return affinity.reshape(z.depth, z.deep, z.strip, z.half)


def solution(mesh):
    return jax.shard_map(
        shards,
        mesh=mesh,
        in_specs=(P("zs", "vol", None), P(), P(), P(), P(), P(), P(), P(), P()),
        out_specs=P(None, None, ("vol", "zs"), None),
        check_vma=False,
    )
```

```python
import functools

import jax
import jax.numpy as jnp
from jax import lax
from jax.experimental import pallas as pl
from jax.experimental.pallas import tpu as pltpu
from jax.sharding import PartitionSpec as P

TILE = 16
SHIFTS = ((1, 2, 0, None), (0, 1, None, 2))
F32 = jnp.float32
BF16 = jnp.bfloat16


def iota(shape, dim):
    return lax.broadcasted_iota(jnp.int32, shape, dim)


def ceil_to(value, step):
    return -(-value // step) * step


def div(value, by):
    if by & (by - 1) == 0:
        return lax.shift_right_logical(value, by.bit_length() - 1)
    return lax.shift_right_logical(value * (-(-65536 // by)), 16)


def one_hot(condition):
    return jnp.where(condition, 1.0, 0.0).astype(BF16)


def nt_dot(lhs, rhs):
    return lax.dot_general(lhs, rhs, (((1,), (1,)), ((), ())), preferred_element_type=F32)


def nn_dot(lhs, rhs):
    return jnp.dot(lhs, rhs, preferred_element_type=F32)


class Sizes:
    def __init__(self, volume, first_weight, reduce_conv_weight, vols, members):
        self.depth = volume.shape[0] * members
        self.cols = volume.shape[2]
        self.half = self.cols // 2
        self.fine_rows = volume.shape[1] * vols
        self.rows = volume.shape[1]
        self.strip = volume.shape[1] // 2 // members
        self.chan = first_weight.shape[1]
        self.deep = reduce_conv_weight.shape[2]
        self.coarse_rows = self.strip + 2
        self.second_rows = 2 * self.coarse_rows
        self.first_rows = self.second_rows + 2
        self.window = self.first_rows + 2
        self.pieces = self.window // 4
        self.lines = ceil_to(self.window, TILE)
        self.ones1 = self.first_rows * self.chan
        self.m1 = ceil_to(self.ones1 + 3, TILE)
        self.m2 = self.second_rows * self.chan
        self.m3 = self.coarse_rows * self.deep
        self.m4 = self.strip * self.deep

    def base(self, member):
        return 2 * self.strip * member - 4


def sort_kernel(z, own_ref, sort_ref, sorted_ref):
    core = lax.rem(lax.axis_index("vol"), 2)
    shape = (z.cols, z.half)
    sort = one_hot(iota(shape, 0) == 2 * iota(shape, 1) + core)
    sort_ref[...] = sort
    for s in range(own_ref.shape[0]):
        sorted_ref[s] = nn_dot(own_ref[s], sort)


def pack_kernel(z, chips, members, own_ref, sort_ref, other_ref, packed_ref):
    vol = lax.axis_index("vol")
    chip = lax.div(vol, 2)
    first_core = vol - 2 * chip == 0
    packed_ref[...] = jnp.zeros(packed_ref.shape, BF16)
    slices = own_ref.shape[0]
    empty = jnp.zeros((4, z.half), BF16)
    for s in range(slices):
        own, other = own_ref[s], nn_dot(other_ref[s], sort_ref[...])
        lines = stacked([jnp.where(first_core, own, other), jnp.where(first_core, other, own)])
        pieces = [lines[row : row + 4].astype(BF16) for row in range(0, 2 * z.rows, 4)]

        def put(to, first):
            for piece in range(z.pieces):
                at = first // 4 + piece
                value = pieces[at] if 0 <= at < len(pieces) else empty
                packed_ref[to * slices + s, :, piece * z.half : (piece + 1) * z.half] = value

        for core in range(2):
            for member in range(members):
                put((2 * chip + core) * members + member, core * z.rows + z.base(member))

        @pl.when(chip < chips - 1)
        def _():
            put(2 * (chip + 1) * members, 2 * z.rows - 4)

        @pl.when(chip > 0)
        def _():
            put(2 * chip * members - 1, 4 - z.window)


def prepare_kernel(
    z, members, w1_ref, b1_ref, w2_ref, b2_ref, w3_ref, b3_ref, w4_ref, b4_ref,
    k1_ref, k2_ref, k3_ref, k4_ref,
):
    member = lax.axis_index("zs")
    start = (lax.axis_index("vol") * members + member) * (2 * z.strip)
    def spread(rows, offsets, period, stretch):
        row = div(iota((rows, period), 0), stretch)
        at = row - div(row, period) * period
        picked = jnp.where(at == iota((rows, period), 1), offsets, 0.0)
        return jnp.sum(picked, axis=1, keepdims=True)

    def bias_terms(column, at):
        high = column.astype(BF16).astype(F32)
        middle = (column - high).astype(BF16).astype(F32)
        low = column - high - middle
        return jnp.where(at == 0, high, jnp.where(at == 1, middle, jnp.where(at == 2, low, 0.0)))

    row = iota((z.m1, z.chan), 0)
    pick = one_hot(row - div(row, z.chan) * z.chan == iota((z.m1, z.chan), 1))
    taps = nt_dot(pick, w1_ref[...]).astype(BF16)
    shape = (z.m1, 4 * z.lines)
    x = div(iota(shape, 0), z.chan)
    col = iota(shape, 1)
    line = col - div(col, z.lines) * z.lines
    inside = (start - 3 + x >= 0) & (start - 3 + x < z.fine_rows) & (x < z.first_rows)
    block = div(iota((9, 4 * z.lines), 1), z.lines)
    narrow = (z.m1, TILE)
    row, col = iota(narrow, 0), iota(narrow, 1)
    narrow_x = div(row, z.chan)
    narrow_inside = (start - 3 + narrow_x >= 0) & (start - 3 + narrow_x < z.fine_rows)
    bias = jnp.where(narrow_inside, bias_terms(spread(z.m1, b1_ref[...], z.chan, 1), col), 0.0)
    ones = jnp.where((row < z.ones1 + 3) & (col == 0), 1.0, 0.0)
    bias = jnp.where(row < z.ones1, bias, ones).astype(BF16)
    for parity, shifts in enumerate(SHIFTS):
        shift = jnp.full(block.shape, 9, jnp.int32)
        for number, value in enumerate(shifts):
            if value is not None:
                shift = jnp.where(block == number, value, shift)
        total = jnp.zeros(shape, F32)
        for i in range(3):
            level = nn_dot(taps, one_hot(iota(block.shape, 0) == 3 * i + shift))
            total += jnp.where(inside & (line == x + i), level, 0.0)
        k1_ref[parity * z.m1 : (parity + 1) * z.m1, : 4 * z.lines] = total.astype(BF16)
        k1_ref[parity * z.m1 : (parity + 1) * z.m1, 4 * z.lines :] = bias

    row = iota((z.m2, z.chan), 0)
    pick = one_hot(row - div(row, z.chan) * z.chan == iota((z.m2, z.chan), 1))
    col = iota((z.chan, z.m1), 1)
    widen = one_hot(col - div(col, z.chan) * z.chan == iota((z.chan, z.m1), 0))
    shape = (z.m2, z.m1)
    lag = div(iota(shape, 1), z.chan) - div(iota(shape, 0), z.chan)
    bias = bias_terms(spread(z.m2, b2_ref[...], z.chan, 1), iota(shape, 1) - z.ones1)
    for s in range(3):
        total = bias if s == 1 else jnp.zeros(shape, F32)
        for i in range(3):
            level = nn_dot(nt_dot(pick, w2_ref[3 * i + s]).astype(BF16), widen)
            total += jnp.where(lag == i, level, 0.0)
        total = total.astype(BF16)
        for parity, shifts in enumerate(SHIFTS):
            at = shifts.index(s)
            k2_ref[parity * z.m2 : (parity + 1) * z.m2, at * z.m1 : (at + 1) * z.m1] = total
    for parity, shifts in enumerate(SHIFTS):
        at = shifts.index(None)
        k2_ref[parity * z.m2 : (parity + 1) * z.m2, at * z.m1 : (at + 1) * z.m1] = jnp.zeros(shape, BF16)

    row = iota((z.m3, z.deep), 0)
    u = div(row, z.deep)
    pick = one_hot(row - u * z.deep == iota((z.m3, z.deep), 1))
    col = iota((z.chan, z.m2), 1)
    widen = one_hot(col - div(col, z.chan) * z.chan == iota((z.chan, z.m2), 0))
    shape = (z.m3, z.m2)
    u = div(iota(shape, 0), z.deep)
    lag = div(iota(shape, 1), z.chan) - 2 * u
    inside = (start + 2 * u >= 2) & (start + 2 * u < z.fine_rows + 2)
    for b in range(2):
        total = jnp.zeros(shape, F32)
        for a in range(2):
            level = nn_dot(nt_dot(pick, w3_ref[2 * a + b]).astype(BF16), widen)
            total += jnp.where(inside & (lag == a), level, 0.0)
        k3_ref[:, b * z.m2 : (b + 1) * z.m2] = total.astype(BF16)
    shape = (z.m3, TILE)
    u = div(iota(shape, 0), z.deep)
    inside = (start + 2 * u >= 2) & (start + 2 * u < z.fine_rows + 2)
    bias = bias_terms(spread(z.m3, b3_ref[...], z.deep, 1), iota(shape, 1))
    k3_ref[:, 2 * z.m2 :] = jnp.where(inside, bias, 0.0).astype(BF16)

    row = iota((z.m4, z.deep), 0)
    pick = one_hot(div(row, z.strip) == iota((z.m4, z.deep), 1))
    col = iota((z.deep, z.m3), 1)
    widen = one_hot(col - div(col, z.deep) * z.deep == iota((z.deep, z.m3), 0))
    shape = (z.m4, z.m3)
    row = iota(shape, 0)
    lag = div(iota(shape, 1), z.deep) - (row - div(row, z.strip) * z.strip)
    for i in range(3):
        for s in range(3):
            total = jnp.zeros(shape, F32)
            for j in range(3):
                level = nn_dot(nt_dot(pick, w4_ref[9 * i + 3 * j + s]).astype(BF16), widen)
                total += jnp.where(lag == j, level, 0.0)
            k4_ref[i * z.m4 : (i + 1) * z.m4, s * z.m3 : (s + 1) * z.m3] = total.astype(BF16)
    shape = (z.m4, TILE)
    bias = bias_terms(spread(z.m4, b4_ref[...], z.deep, z.strip), iota(shape, 1))
    for i in range(3):
        terms = bias if i == 1 else jnp.zeros(shape, F32)
        k4_ref[i * z.m4 : (i + 1) * z.m4, 3 * z.m3 :] = terms.astype(BF16)


def relu(value):
    return jnp.maximum(value.astype(BF16), 0)


def side_by_side(values):
    return jnp.concatenate(values, axis=1)


def stacked(values):
    return jnp.concatenate(values, axis=0)


def moved(value, by, lanes):
    width = value.shape[1]
    turned = pltpu.roll(value, by % width, axis=1)
    edge = 0 if by == 1 else width - 1
    return jnp.where(lanes == edge, jnp.zeros_like(turned), turned)


def main_kernel(
    z, chips, got_ref, k1_ref, k2_ref, k3_ref, k4_ref, out_ref, coarse,
):
    chip = lax.div(lax.axis_index("vol"), 2)
    sources = [chip]
    if chips > 1:
        sources.append(lax.rem(chip + 1, chips))
    if chips > 2:
        sources.append(lax.rem(chip + chips - 1, chips))
    group = min(z.depth, 8)
    groups = z.depth // group
    n = z.half
    ones = jnp.ones((TILE, z.cols), BF16)
    blanks = [jnp.zeros((z.lines - z.window, n), F32)] if z.lines > z.window else []
    lanes0 = iota((z.lines, n), 1)
    lanes1 = iota((z.m1, n), 1)
    lanes3 = iota((z.m3, n), 1)
    if groups > 1:
        coarse[0] = jnp.zeros((z.m3, n), BF16)
        coarse[z.depth + 1] = jnp.zeros((z.m3, n), BF16)

    def blocks(evens, odds, lanes):
        odds_right = [moved(odd, 1, lanes) for odd in odds]
        evens_left = [moved(even, -1, lanes) for even in evens]
        return [side_by_side(pair) for pair in (evens, odds, odds_right, evens_left)]

    def lines_of(k, core):
        window = sum(got_ref[source, core, k].astype(F32) for source in sources)
        return stacked([window[:, piece * n : (piece + 1) * n] for piece in range(z.pieces)] + blanks)

    def leading(base):
        fields = []
        for k in range(0, group, 2):
            evens, odds = ([lines_of(base + k, core), lines_of(base + k + 1, core)] for core in range(2))
            fields.append(stacked([stacked(blocks(evens, odds, lanes0)).astype(BF16), ones]))
        firsts = [relu(nn_dot(k1_ref[...], field)) for field in fields]
        fields = []
        for first in firsts:
            even, odd = first[: z.m1], first[z.m1 :]
            moves = blocks([even[:, :n], even[:, n:]], [odd[:, :n], odd[:, n:]], lanes1)[2:]
            fields.append(stacked([first] + moves))
        seconds = [relu(nn_dot(k2_ref[...], field)) for field in fields]
        for k, second in enumerate(seconds):
            reduced = relu(nn_dot(k3_ref[...], stacked([second, ones])))
            coarse[base + 2 * k + 1] = reduced[:, :n]
            coarse[base + 2 * k + 2] = reduced[:, n:]

    def trailing(base):
        planes = list(range(-1, group + 1)) if groups > 1 else list(range(group))
        totals = [None] * group
        for q in range(0, len(planes), 2):
            pair = planes[q : q + 2]
            fields = []
            for k in pair:
                plane = coarse[base + k + 1]
                fields.append(stacked([moved(plane, 1, lanes3), plane, moved(plane, -1, lanes3), ones[:, :n]]))
            terms = nn_dot(k4_ref[...], side_by_side(fields))
            for side, k in enumerate(pair):
                for i in range(3):
                    to = k + 1 - i
                    if 0 <= to < group:
                        term = terms[i * z.m4 : (i + 1) * z.m4, side * n : (side + 1) * n]
                        totals[to] = term if totals[to] is None else totals[to] + term
        for k in range(group):
            out_ref[base + k] = relu(totals[k])

    if groups == 1:
        leading(0)
        trailing(0)
    else:
        pl.loop(0, groups)(lambda g: leading(g * group))
        pl.loop(0, groups)(lambda g: trailing(g * group))


def shards(
    volume, first_weight, first_offset, second_weight, second_offset,
    reduce_conv_weight, reduce_conv_bias, deep_weight, deep_offset,
):
    vols, members = lax.axis_size("vol"), lax.axis_size("zs")
    z = Sizes(volume, first_weight, reduce_conv_weight, vols, members)
    slices = volume.shape[0]
    vmem = pl.BlockSpec(memory_space=pltpu.VMEM)
    like = jax.ShapeDtypeStruct
    chips = vols // 2
    other = lax.ppermute(volume, "vol", [(v, v ^ 1) for v in range(vols)])
    sort, own = pl.pallas_call(
        functools.partial(sort_kernel, z),
        out_shape=(like((z.cols, z.half), BF16), like((slices, z.rows, z.half), F32)),
        in_specs=[vmem],
        out_specs=(vmem,) * 2,
        compiler_params=pltpu.CompilerParams(vmem_limit_bytes=16 * 1024 * 1024),
        cost_estimate=pl.CostEstimate(flops=5_000_000, bytes_accessed=100_000, transcendentals=0),
        name="sort",
    )(volume)
    packed = pl.pallas_call(
        functools.partial(pack_kernel, z, chips, members),
        out_shape=like((vols * members * slices, 4, z.pieces * z.half), BF16),
        in_specs=[vmem] * 3,
        out_specs=vmem,
        compiler_params=pltpu.CompilerParams(vmem_limit_bytes=16 * 1024 * 1024),
        name="pack",
    )(own, sort, other)
    packed, *parameters = lax.optimization_barrier((
        packed, first_weight, first_offset, second_weight, second_offset,
        reduce_conv_weight, reduce_conv_bias, deep_weight, deep_offset,
    ))
    got = lax.all_to_all(packed, ("vol", "zs"), split_axis=0, concat_axis=0, tiled=True)
    got = got.reshape(chips, 2, z.depth, 4, z.pieces * z.half)
    prepared = pl.pallas_call(
        functools.partial(prepare_kernel, z, members),
        out_shape=(
            like((2 * z.m1, 4 * z.lines + TILE), BF16),
            like((2 * z.m2, 4 * z.m1), BF16),
            like((z.m3, 2 * z.m2 + TILE), BF16),
            like((3 * z.m4, 3 * z.m3 + TILE), BF16),
        ),
        in_specs=[vmem] * 8,
        out_specs=(vmem,) * 4,
        compiler_params=pltpu.CompilerParams(vmem_limit_bytes=16 * 1024 * 1024),
        cost_estimate=pl.CostEstimate(flops=50_000_000, bytes_accessed=1_000_000, transcendentals=0),
        name="prepare",
    )(
        *(value[None] if value.ndim == 1 else value for value in parameters)
    )
    affinity = pl.pallas_call(
        functools.partial(main_kernel, z, chips),
        out_shape=like((z.depth, z.m4, z.half), BF16),
        in_specs=[vmem] * 5,
        out_specs=vmem,
        scratch_shapes=[
            pltpu.VMEM((z.depth + 2, z.m3, z.half), BF16),
        ],
        compiler_params=pltpu.CompilerParams(vmem_limit_bytes=32 * 1024 * 1024),
        cost_estimate=pl.CostEstimate(flops=2_000_000_000, bytes_accessed=2_000_000, transcendentals=0),
        name="encode",
    )(got, *prepared)
    return affinity.reshape(z.depth, z.deep, z.strip, z.half)


def solution(mesh):
    return jax.shard_map(
        shards,
        mesh=mesh,
        in_specs=(P("zs", "vol", None), P(), P(), P(), P(), P(), P(), P(), P()),
        out_specs=P(None, None, ("vol", "zs"), None),
        check_vma=False,
    )
```

```python
import functools

import jax
import jax.numpy as jnp
from jax import lax
from jax.experimental import pallas as pl
from jax.experimental.pallas import tpu as pltpu
from jax.sharding import PartitionSpec as P

TILE = 16
SHIFTS = ((1, 2, 0, None), (0, 1, None, 2))
F32 = jnp.float32
BF16 = jnp.bfloat16


def iota(shape, dim):
    return lax.broadcasted_iota(jnp.int32, shape, dim)


def ceil_to(value, step):
    return -(-value // step) * step


def div(value, by):
    if by & (by - 1) == 0:
        return lax.shift_right_logical(value, by.bit_length() - 1)
    return lax.shift_right_logical(value * (-(-65536 // by)), 16)


def one_hot(condition):
    return jnp.where(condition, 1.0, 0.0).astype(BF16)


def nt_dot(lhs, rhs):
    return lax.dot_general(lhs, rhs, (((1,), (1,)), ((), ())), preferred_element_type=F32)


def nn_dot(lhs, rhs):
    return jnp.dot(lhs, rhs, preferred_element_type=F32)


class Sizes:
    def __init__(self, volume, first_weight, reduce_conv_weight, vols, members):
        self.depth = volume.shape[0] * members
        self.cols = volume.shape[2]
        self.half = self.cols // 2
        self.fine_rows = volume.shape[1] * vols
        self.rows = volume.shape[1]
        self.strip = volume.shape[1] // 2 // members
        self.chan = first_weight.shape[1]
        self.deep = reduce_conv_weight.shape[2]
        self.coarse_rows = self.strip + 2
        self.second_rows = 2 * self.coarse_rows
        self.first_rows = self.second_rows + 2
        self.window = self.first_rows + 2
        self.pieces = self.window // 4
        self.lines = ceil_to(self.window, TILE)
        self.ones1 = self.first_rows * self.chan
        self.m1 = ceil_to(self.ones1 + 3, TILE)
        self.m2 = self.second_rows * self.chan
        self.m3 = self.coarse_rows * self.deep
        self.m4 = self.strip * self.deep

    def base(self, member):
        return 2 * self.strip * member - 4


def sort_kernel(z, own_ref, sort_ref, sorted_ref):
    core = lax.rem(lax.axis_index("vol"), 2)
    shape = (z.cols, z.half)
    sort = one_hot(iota(shape, 0) == 2 * iota(shape, 1) + core)
    sort_ref[...] = sort
    for s in range(own_ref.shape[0]):
        sorted_ref[s] = nn_dot(own_ref[s], sort)


def pack_kernel(z, chips, members, own_ref, sort_ref, other_ref, packed_ref):
    vol = lax.axis_index("vol")
    chip = lax.div(vol, 2)
    first_core = vol - 2 * chip == 0
    packed_ref[...] = jnp.zeros(packed_ref.shape, BF16)
    slices = own_ref.shape[0]
    empty = jnp.zeros((4, z.half), BF16)
    for s in range(slices):
        own, other = own_ref[s], nn_dot(other_ref[s], sort_ref[...])
        lines = stacked([jnp.where(first_core, own, other), jnp.where(first_core, other, own)])
        pieces = [lines[row : row + 4].astype(BF16) for row in range(0, 2 * z.rows, 4)]

        def put(to, first):
            for piece in range(z.pieces):
                at = first // 4 + piece
                value = pieces[at] if 0 <= at < len(pieces) else empty
                packed_ref[to * slices + s, :, piece * z.half : (piece + 1) * z.half] = value

        for core in range(2):
            for member in range(members):
                put((2 * chip + core) * members + member, core * z.rows + z.base(member))

        @pl.when(chip < chips - 1)
        def _():
            put(2 * (chip + 1) * members, 2 * z.rows - 4)

        @pl.when(chip > 0)
        def _():
            put(2 * chip * members - 1, 4 - z.window)


def prepare_kernel(
    z, members, w1_ref, b1_ref, w2_ref, b2_ref, w3_ref, b3_ref, w4_ref, b4_ref,
    k1_ref, k2_ref, k3_ref, k4_ref,
):
    member = lax.axis_index("zs")
    start = (lax.axis_index("vol") * members + member) * (2 * z.strip)
    def spread(rows, offsets, period, stretch):
        row = div(iota((rows, period), 0), stretch)
        at = row - div(row, period) * period
        picked = jnp.where(at == iota((rows, period), 1), offsets, 0.0)
        return jnp.sum(picked, axis=1, keepdims=True)

    def bias_terms(column, at):
        high = column.astype(BF16).astype(F32)
        middle = (column - high).astype(BF16).astype(F32)
        low = column - high - middle
        return jnp.where(at == 0, high, jnp.where(at == 1, middle, jnp.where(at == 2, low, 0.0)))

    row = iota((z.m1, z.chan), 0)
    pick = one_hot(row - div(row, z.chan) * z.chan == iota((z.m1, z.chan), 1))
    taps = nt_dot(pick, w1_ref[...]).astype(BF16)
    shape = (z.m1, 4 * z.lines)
    x = div(iota(shape, 0), z.chan)
    col = iota(shape, 1)
    line = col - div(col, z.lines) * z.lines
    inside = (start - 3 + x >= 0) & (start - 3 + x < z.fine_rows) & (x < z.first_rows)
    block = div(iota((9, 4 * z.lines), 1), z.lines)
    narrow = (z.m1, TILE)
    row, col = iota(narrow, 0), iota(narrow, 1)
    narrow_x = div(row, z.chan)
    narrow_inside = (start - 3 + narrow_x >= 0) & (start - 3 + narrow_x < z.fine_rows)
    bias = jnp.where(narrow_inside, bias_terms(spread(z.m1, b1_ref[...], z.chan, 1), col), 0.0)
    ones = jnp.where((row < z.ones1 + 3) & (col == 0), 1.0, 0.0)
    bias = jnp.where(row < z.ones1, bias, ones).astype(BF16)
    for parity, shifts in enumerate(SHIFTS):
        shift = jnp.full(block.shape, 9, jnp.int32)
        for number, value in enumerate(shifts):
            if value is not None:
                shift = jnp.where(block == number, value, shift)
        total = jnp.zeros(shape, F32)
        for i in range(3):
            level = nn_dot(taps, one_hot(iota(block.shape, 0) == 3 * i + shift))
            total += jnp.where(inside & (line == x + i), level, 0.0)
        k1_ref[parity * z.m1 : (parity + 1) * z.m1, : 4 * z.lines] = total.astype(BF16)
        k1_ref[parity * z.m1 : (parity + 1) * z.m1, 4 * z.lines :] = bias

    row = iota((z.m2, z.chan), 0)
    pick = one_hot(row - div(row, z.chan) * z.chan == iota((z.m2, z.chan), 1))
    col = iota((z.chan, z.m1), 1)
    widen = one_hot(col - div(col, z.chan) * z.chan == iota((z.chan, z.m1), 0))
    shape = (z.m2, z.m1)
    lag = div(iota(shape, 1), z.chan) - div(iota(shape, 0), z.chan)
    bias = bias_terms(spread(z.m2, b2_ref[...], z.chan, 1), iota(shape, 1) - z.ones1)
    for s in range(3):
        total = bias if s == 1 else jnp.zeros(shape, F32)
        for i in range(3):
            level = nn_dot(nt_dot(pick, w2_ref[3 * i + s]).astype(BF16), widen)
            total += jnp.where(lag == i, level, 0.0)
        total = total.astype(BF16)
        for parity, shifts in enumerate(SHIFTS):
            at = shifts.index(s)
            k2_ref[parity * z.m2 : (parity + 1) * z.m2, at * z.m1 : (at + 1) * z.m1] = total
    for parity, shifts in enumerate(SHIFTS):
        at = shifts.index(None)
        k2_ref[parity * z.m2 : (parity + 1) * z.m2, at * z.m1 : (at + 1) * z.m1] = jnp.zeros(shape, BF16)

    row = iota((z.m3, z.deep), 0)
    u = div(row, z.deep)
    pick = one_hot(row - u * z.deep == iota((z.m3, z.deep), 1))
    col = iota((z.chan, z.m2), 1)
    widen = one_hot(col - div(col, z.chan) * z.chan == iota((z.chan, z.m2), 0))
    shape = (z.m3, z.m2)
    u = div(iota(shape, 0), z.deep)
    lag = div(iota(shape, 1), z.chan) - 2 * u
    inside = (start + 2 * u >= 2) & (start + 2 * u < z.fine_rows + 2)
    for b in range(2):
        total = jnp.zeros(shape, F32)
        for a in range(2):
            level = nn_dot(nt_dot(pick, w3_ref[2 * a + b]).astype(BF16), widen)
            total += jnp.where(inside & (lag == a), level, 0.0)
        k3_ref[:, b * z.m2 : (b + 1) * z.m2] = total.astype(BF16)
    shape = (z.m3, TILE)
    u = div(iota(shape, 0), z.deep)
    inside = (start + 2 * u >= 2) & (start + 2 * u < z.fine_rows + 2)
    bias = bias_terms(spread(z.m3, b3_ref[...], z.deep, 1), iota(shape, 1))
    k3_ref[:, 2 * z.m2 :] = jnp.where(inside, bias, 0.0).astype(BF16)

    row = iota((z.m4, z.deep), 0)
    pick = one_hot(div(row, z.strip) == iota((z.m4, z.deep), 1))
    col = iota((z.deep, z.m3), 1)
    widen = one_hot(col - div(col, z.deep) * z.deep == iota((z.deep, z.m3), 0))
    shape = (z.m4, z.m3)
    row = iota(shape, 0)
    lag = div(iota(shape, 1), z.deep) - (row - div(row, z.strip) * z.strip)
    for i in range(3):
        for s in range(3):
            total = jnp.zeros(shape, F32)
            for j in range(3):
                level = nn_dot(nt_dot(pick, w4_ref[9 * i + 3 * j + s]).astype(BF16), widen)
                total += jnp.where(lag == j, level, 0.0)
            k4_ref[i * z.m4 : (i + 1) * z.m4, s * z.m3 : (s + 1) * z.m3] = total.astype(BF16)
    shape = (z.m4, TILE)
    bias = bias_terms(spread(z.m4, b4_ref[...], z.deep, z.strip), iota(shape, 1))
    for i in range(3):
        terms = bias if i == 1 else jnp.zeros(shape, F32)
        k4_ref[i * z.m4 : (i + 1) * z.m4, 3 * z.m3 :] = terms.astype(BF16)


def relu(value):
    return jnp.maximum(value.astype(BF16), 0)


def side_by_side(values):
    return jnp.concatenate(values, axis=1)


def stacked(values):
    return jnp.concatenate(values, axis=0)


def moved(value, by, lanes):
    width = value.shape[1]
    turned = pltpu.roll(value, by % width, axis=1)
    edge = 0 if by == 1 else width - 1
    return jnp.where(lanes == edge, jnp.zeros_like(turned), turned)


def main_kernel(
    z, chips, got_ref, k1_ref, k2_ref, k3_ref, k4_ref, out_ref, coarse,
):
    chip = lax.div(lax.axis_index("vol"), 2)
    sources = [chip]
    if chips > 1:
        sources.append(lax.rem(chip + 1, chips))
    if chips > 2:
        sources.append(lax.rem(chip + chips - 1, chips))
    group = min(z.depth, 8)
    groups = z.depth // group
    n = z.half
    ones = jnp.ones((TILE, z.cols), BF16)
    blanks = [jnp.zeros((z.lines - z.window, n), F32)] if z.lines > z.window else []
    lanes0 = iota((z.lines, n), 1)
    lanes1 = iota((z.m1, n), 1)
    lanes3 = iota((z.m3, n), 1)

    def blocks(evens, odds, lanes):
        odds_right = [moved(odd, 1, lanes) for odd in odds]
        evens_left = [moved(even, -1, lanes) for even in evens]
        return [side_by_side(pair) for pair in (evens, odds, odds_right, evens_left)]

    def lines_of(k, core):
        window = sum(got_ref[source, core, k].astype(F32) for source in sources)
        lines = [window[:, piece * n : (piece + 1) * n] for piece in range(z.pieces)]
        return stacked(lines + blanks).astype(BF16)

    def leading(base):
        fields = []
        for k in range(0, group, 2):
            evens, odds = ([lines_of(base + k, core), lines_of(base + k + 1, core)] for core in range(2))
            fields.append(stacked(blocks(evens, odds, lanes0) + [ones]))
        firsts = [relu(nn_dot(k1_ref[...], field)) for field in fields]
        fields = []
        for first in firsts:
            even, odd = first[: z.m1], first[z.m1 :]
            moves = blocks([even[:, :n], even[:, n:]], [odd[:, :n], odd[:, n:]], lanes1)[2:]
            fields.append(stacked([first] + moves))
        seconds = [relu(nn_dot(k2_ref[...], field)) for field in fields]
        planes = []
        for second in seconds:
            reduced = relu(nn_dot(k3_ref[...], stacked([second, ones])))
            planes += [reduced[:, :n], reduced[:, n:]]
        return planes

    def trailing(base, planes, values):
        totals = [None] * group
        for q in range(0, len(planes), 2):
            pair = planes[q : q + 2]
            fields = []
            for k in pair:
                plane = values[k]
                fields.append(stacked([moved(plane, 1, lanes3), plane, moved(plane, -1, lanes3), ones[:, :n]]))
            terms = nn_dot(k4_ref[...], side_by_side(fields))
            for side, k in enumerate(pair):
                for i in range(3):
                    to = k + 1 - i
                    if 0 <= to < group:
                        term = terms[i * z.m4 : (i + 1) * z.m4, side * n : (side + 1) * n]
                        totals[to] = term if totals[to] is None else totals[to] + term
        for k in range(group):
            out_ref[base + k] = relu(totals[k])

    if groups == 1:
        trailing(0, list(range(group)), leading(0))
        return

    coarse[0] = jnp.zeros((z.m3, n), BF16)
    coarse[z.depth + 1] = jnp.zeros((z.m3, n), BF16)

    @pl.loop(0, groups)
    def _(g):
        for k, plane in enumerate(leading(g * group)):
            coarse[g * group + k + 1] = plane

    @pl.loop(0, groups)
    def _(g):
        around = list(range(-1, group + 1))
        trailing(g * group, around, {k: coarse[g * group + k + 1] for k in around})


def shards(
    volume, first_weight, first_offset, second_weight, second_offset,
    reduce_conv_weight, reduce_conv_bias, deep_weight, deep_offset,
):
    vols, members = lax.axis_size("vol"), lax.axis_size("zs")
    z = Sizes(volume, first_weight, reduce_conv_weight, vols, members)
    slices = volume.shape[0]
    vmem = pl.BlockSpec(memory_space=pltpu.VMEM)
    like = jax.ShapeDtypeStruct
    chips = vols // 2
    other = lax.ppermute(volume, "vol", [(v, v ^ 1) for v in range(vols)])
    sort, own = pl.pallas_call(
        functools.partial(sort_kernel, z),
        out_shape=(like((z.cols, z.half), BF16), like((slices, z.rows, z.half), F32)),
        in_specs=[vmem],
        out_specs=(vmem,) * 2,
        compiler_params=pltpu.CompilerParams(vmem_limit_bytes=16 * 1024 * 1024),
        cost_estimate=pl.CostEstimate(flops=5_000_000, bytes_accessed=100_000, transcendentals=0),
        name="sort",
    )(volume)
    packed = pl.pallas_call(
        functools.partial(pack_kernel, z, chips, members),
        out_shape=like((vols * members * slices, 4, z.pieces * z.half), BF16),
        in_specs=[vmem] * 3,
        out_specs=vmem,
        compiler_params=pltpu.CompilerParams(vmem_limit_bytes=16 * 1024 * 1024),
        name="pack",
    )(own, sort, other)
    packed, *parameters = lax.optimization_barrier((
        packed, first_weight, first_offset, second_weight, second_offset,
        reduce_conv_weight, reduce_conv_bias, deep_weight, deep_offset,
    ))
    got = lax.all_to_all(packed, ("vol", "zs"), split_axis=0, concat_axis=0, tiled=True)
    got = got.reshape(chips, 2, z.depth, 4, z.pieces * z.half)
    prepared = pl.pallas_call(
        functools.partial(prepare_kernel, z, members),
        out_shape=(
            like((2 * z.m1, 4 * z.lines + TILE), BF16),
            like((2 * z.m2, 4 * z.m1), BF16),
            like((z.m3, 2 * z.m2 + TILE), BF16),
            like((3 * z.m4, 3 * z.m3 + TILE), BF16),
        ),
        in_specs=[vmem] * 8,
        out_specs=(vmem,) * 4,
        compiler_params=pltpu.CompilerParams(vmem_limit_bytes=16 * 1024 * 1024),
        cost_estimate=pl.CostEstimate(flops=50_000_000, bytes_accessed=1_000_000, transcendentals=0),
        name="prepare",
    )(
        *(value[None] if value.ndim == 1 else value for value in parameters)
    )
    affinity = pl.pallas_call(
        functools.partial(main_kernel, z, chips),
        out_shape=like((z.depth, z.m4, z.half), BF16),
        in_specs=[vmem] * 5,
        out_specs=vmem,
        scratch_shapes=[
            pltpu.VMEM((z.depth + 2, z.m3, z.half), BF16),
        ],
        compiler_params=pltpu.CompilerParams(vmem_limit_bytes=32 * 1024 * 1024),
        cost_estimate=pl.CostEstimate(flops=2_000_000_000, bytes_accessed=2_000_000, transcendentals=0),
        name="encode",
    )(got, *prepared)
    return affinity.reshape(z.depth, z.deep, z.strip, z.half)


def solution(mesh):
    return jax.shard_map(
        shards,
        mesh=mesh,
        in_specs=(P("zs", "vol", None), P(), P(), P(), P(), P(), P(), P(), P()),
        out_specs=P(None, None, ("vol", "zs"), None),
        check_vma=False,
    )
```

```python
import functools

import jax
import jax.numpy as jnp
from jax import lax
from jax.experimental import pallas as pl
from jax.experimental.pallas import tpu as pltpu
from jax.sharding import PartitionSpec as P

TILE = 16
SHIFTS = ((1, 2, 0, None), (0, 1, None, 2))
F32 = jnp.float32
BF16 = jnp.bfloat16


def iota(shape, dim):
    return lax.broadcasted_iota(jnp.int32, shape, dim)


def ceil_to(value, step):
    return -(-value // step) * step


def div(value, by):
    if by & (by - 1) == 0:
        return lax.shift_right_logical(value, by.bit_length() - 1)
    return lax.shift_right_logical(value * (-(-65536 // by)), 16)


def one_hot(condition):
    return jnp.where(condition, 1.0, 0.0).astype(BF16)


def nt_dot(lhs, rhs):
    return lax.dot_general(lhs, rhs, (((1,), (1,)), ((), ())), preferred_element_type=F32)


def nn_dot(lhs, rhs):
    return jnp.dot(lhs, rhs, preferred_element_type=F32)


class Sizes:
    def __init__(self, volume, first_weight, reduce_conv_weight, vols, members):
        self.depth = volume.shape[0] * members
        self.cols = volume.shape[2]
        self.half = self.cols // 2
        self.fine_rows = volume.shape[1] * vols
        self.rows = volume.shape[1]
        self.strip = volume.shape[1] // 2 // members
        self.chan = first_weight.shape[1]
        self.deep = reduce_conv_weight.shape[2]
        self.coarse_rows = self.strip + 2
        self.second_rows = 2 * self.coarse_rows
        self.first_rows = self.second_rows + 2
        self.window = self.first_rows + 2
        self.pieces = self.window // 4
        self.lines = ceil_to(self.window, TILE)
        self.ones1 = self.first_rows * self.chan
        self.m1 = ceil_to(self.ones1 + 3, TILE)
        self.m2 = self.second_rows * self.chan
        self.m3 = self.coarse_rows * self.deep
        self.m4 = self.strip * self.deep

    def base(self, member):
        return 2 * self.strip * member - 4


def half_of(lines, first_core, z):
    return jnp.where(first_core, lines[:, : z.half], lines[:, z.half :])


def load_kernel(z, volume_ref, own_ref):
    first_core = lax.rem(lax.axis_index("vol"), 2) == 0
    for s in range(volume_ref.shape[0]):
        own_ref[s] = half_of(volume_ref[s].astype(F32), first_core, z)


def pack_kernel(z, chips, members, own_ref, other_ref, packed_ref):
    vol = lax.axis_index("vol")
    chip = lax.div(vol, 2)
    first_core = vol - 2 * chip == 0
    packed_ref[...] = jnp.zeros(packed_ref.shape, BF16)
    slices = own_ref.shape[0]
    empty = jnp.zeros((4, z.half), BF16)
    for s in range(slices):
        own, other = own_ref[s], half_of(other_ref[s].astype(F32), first_core, z)
        lines = stacked([jnp.where(first_core, own, other), jnp.where(first_core, other, own)])
        pieces = [lines[row : row + 4].astype(BF16) for row in range(0, 2 * z.rows, 4)]

        def put(to, first):
            for piece in range(z.pieces):
                at = first // 4 + piece
                value = pieces[at] if 0 <= at < len(pieces) else empty
                packed_ref[to * slices + s, :, piece * z.half : (piece + 1) * z.half] = value

        for core in range(2):
            for member in range(members):
                put((2 * chip + core) * members + member, core * z.rows + z.base(member))

        @pl.when(chip < chips - 1)
        def _():
            put(2 * (chip + 1) * members, 2 * z.rows - 4)

        @pl.when(chip > 0)
        def _():
            put(2 * chip * members - 1, 4 - z.window)


def prepare_kernel(
    z, members, w1_ref, b1_ref, w2_ref, b2_ref, w3_ref, b3_ref, w4_ref, b4_ref,
    sort_ref, k1_ref, k2_ref, k3_ref, k4_ref,
):
    member = lax.axis_index("zs")
    start = (lax.axis_index("vol") * members + member) * (2 * z.strip)
    shape = (z.cols, 4 * z.half)
    col = iota(shape, 1)
    block = div(col, z.half)
    step = jnp.where(block == 0, 0, jnp.where(block == 1, 1, jnp.where(block == 2, -1, 2)))
    sort_ref[...] = one_hot(iota(shape, 0) == 2 * (col - block * z.half) + step)

    def spread(rows, offsets, period, stretch):
        row = div(iota((rows, period), 0), stretch)
        at = row - div(row, period) * period
        picked = jnp.where(at == iota((rows, period), 1), offsets, 0.0)
        return jnp.sum(picked, axis=1, keepdims=True)

    def bias_terms(column, at):
        high = column.astype(BF16).astype(F32)
        middle = (column - high).astype(BF16).astype(F32)
        low = column - high - middle
        return jnp.where(at == 0, high, jnp.where(at == 1, middle, jnp.where(at == 2, low, 0.0)))

    row = iota((z.m1, z.chan), 0)
    pick = one_hot(row - div(row, z.chan) * z.chan == iota((z.m1, z.chan), 1))
    taps = nt_dot(pick, w1_ref[...]).astype(BF16)
    shape = (z.m1, 4 * z.lines)
    x = div(iota(shape, 0), z.chan)
    col = iota(shape, 1)
    line = col - div(col, z.lines) * z.lines
    inside = (start - 3 + x >= 0) & (start - 3 + x < z.fine_rows) & (x < z.first_rows)
    block = div(iota((9, 4 * z.lines), 1), z.lines)
    narrow = (z.m1, TILE)
    row, col = iota(narrow, 0), iota(narrow, 1)
    narrow_x = div(row, z.chan)
    narrow_inside = (start - 3 + narrow_x >= 0) & (start - 3 + narrow_x < z.fine_rows)
    bias = jnp.where(narrow_inside, bias_terms(spread(z.m1, b1_ref[...], z.chan, 1), col), 0.0)
    ones = jnp.where((row < z.ones1 + 3) & (col == 0), 1.0, 0.0)
    bias = jnp.where(row < z.ones1, bias, ones).astype(BF16)
    for parity, shifts in enumerate(SHIFTS):
        shift = jnp.full(block.shape, 9, jnp.int32)
        for number, value in enumerate(shifts):
            if value is not None:
                shift = jnp.where(block == number, value, shift)
        total = jnp.zeros(shape, F32)
        for i in range(3):
            level = nn_dot(taps, one_hot(iota(block.shape, 0) == 3 * i + shift))
            total += jnp.where(inside & (line == x + i), level, 0.0)
        k1_ref[parity * z.m1 : (parity + 1) * z.m1, : 4 * z.lines] = total.astype(BF16)
        k1_ref[parity * z.m1 : (parity + 1) * z.m1, 4 * z.lines :] = bias

    row = iota((z.m2, z.chan), 0)
    pick = one_hot(row - div(row, z.chan) * z.chan == iota((z.m2, z.chan), 1))
    col = iota((z.chan, z.m1), 1)
    widen = one_hot(col - div(col, z.chan) * z.chan == iota((z.chan, z.m1), 0))
    shape = (z.m2, z.m1)
    lag = div(iota(shape, 1), z.chan) - div(iota(shape, 0), z.chan)
    bias = bias_terms(spread(z.m2, b2_ref[...], z.chan, 1), iota(shape, 1) - z.ones1)
    for s in range(3):
        total = bias if s == 1 else jnp.zeros(shape, F32)
        for i in range(3):
            level = nn_dot(nt_dot(pick, w2_ref[3 * i + s]).astype(BF16), widen)
            total += jnp.where(lag == i, level, 0.0)
        total = total.astype(BF16)
        for parity, shifts in enumerate(SHIFTS):
            at = shifts.index(s)
            k2_ref[parity * z.m2 : (parity + 1) * z.m2, at * z.m1 : (at + 1) * z.m1] = total
    for parity, shifts in enumerate(SHIFTS):
        at = shifts.index(None)
        k2_ref[parity * z.m2 : (parity + 1) * z.m2, at * z.m1 : (at + 1) * z.m1] = jnp.zeros(shape, BF16)

    row = iota((z.m3, z.deep), 0)
    u = div(row, z.deep)
    pick = one_hot(row - u * z.deep == iota((z.m3, z.deep), 1))
    col = iota((z.chan, z.m2), 1)
    widen = one_hot(col - div(col, z.chan) * z.chan == iota((z.chan, z.m2), 0))
    shape = (z.m3, z.m2)
    u = div(iota(shape, 0), z.deep)
    lag = div(iota(shape, 1), z.chan) - 2 * u
    inside = (start + 2 * u >= 2) & (start + 2 * u < z.fine_rows + 2)
    for b in range(2):
        total = jnp.zeros(shape, F32)
        for a in range(2):
            level = nn_dot(nt_dot(pick, w3_ref[2 * a + b]).astype(BF16), widen)
            total += jnp.where(inside & (lag == a), level, 0.0)
        k3_ref[:, b * z.m2 : (b + 1) * z.m2] = total.astype(BF16)
    shape = (z.m3, TILE)
    u = div(iota(shape, 0), z.deep)
    inside = (start + 2 * u >= 2) & (start + 2 * u < z.fine_rows + 2)
    bias = bias_terms(spread(z.m3, b3_ref[...], z.deep, 1), iota(shape, 1))
    k3_ref[:, 2 * z.m2 :] = jnp.where(inside, bias, 0.0).astype(BF16)

    row = iota((z.m4, z.deep), 0)
    pick = one_hot(div(row, z.strip) == iota((z.m4, z.deep), 1))
    col = iota((z.deep, z.m3), 1)
    widen = one_hot(col - div(col, z.deep) * z.deep == iota((z.deep, z.m3), 0))
    shape = (z.m4, z.m3)
    row = iota(shape, 0)
    lag = div(iota(shape, 1), z.deep) - (row - div(row, z.strip) * z.strip)
    for i in range(3):
        for s in range(3):
            total = jnp.zeros(shape, F32)
            for j in range(3):
                level = nn_dot(nt_dot(pick, w4_ref[9 * i + 3 * j + s]).astype(BF16), widen)
                total += jnp.where(lag == j, level, 0.0)
            k4_ref[i * z.m4 : (i + 1) * z.m4, s * z.m3 : (s + 1) * z.m3] = total.astype(BF16)
    shape = (z.m4, TILE)
    bias = bias_terms(spread(z.m4, b4_ref[...], z.deep, z.strip), iota(shape, 1))
    for i in range(3):
        terms = bias if i == 1 else jnp.zeros(shape, F32)
        k4_ref[i * z.m4 : (i + 1) * z.m4, 3 * z.m3 :] = terms.astype(BF16)


def relu(value):
    return jnp.maximum(value.astype(BF16), 0)


def side_by_side(values):
    return jnp.concatenate(values, axis=1)


def stacked(values):
    return jnp.concatenate(values, axis=0)


def moved(value, by, lanes):
    width = value.shape[1]
    turned = pltpu.roll(value, by % width, axis=1)
    edge = 0 if by == 1 else width - 1
    return jnp.where(lanes == edge, jnp.zeros_like(turned), turned)


def main_kernel(
    z, chips, got_ref, sort_ref, k1_ref, k2_ref, k3_ref, k4_ref, out_ref, coarse,
):
    chip = lax.div(lax.axis_index("vol"), 2)
    sources = [chip]
    if chips > 1:
        sources.append(lax.rem(chip + 1, chips))
    if chips > 2:
        sources.append(lax.rem(chip + chips - 1, chips))
    group = min(z.depth, 8)
    groups = z.depth // group
    n = z.half
    ones = jnp.ones((TILE, z.cols), BF16)
    blanks = [jnp.zeros((z.lines - z.window, n), F32)] if z.lines > z.window else []
    lanes1 = iota((z.m1, n), 1)
    lanes3 = iota((z.m3, n), 1)
    if groups > 1:
        coarse[0] = jnp.zeros((z.m3, n), BF16)
        coarse[z.depth + 1] = jnp.zeros((z.m3, n), BF16)

    def blocks(evens, odds, lanes):
        odds_right = [moved(odd, 1, lanes) for odd in odds]
        evens_left = [moved(even, -1, lanes) for even in evens]
        return [side_by_side(pair) for pair in (evens, odds, odds_right, evens_left)]

    def lines_of(k, core):
        window = sum(got_ref[source, core, k].astype(F32) for source in sources)
        lines = [window[:, piece * n : (piece + 1) * n] for piece in range(z.pieces)]
        return stacked(lines + blanks).astype(BF16)

    def leading(base):
        lines = stacked([side_by_side([lines_of(base + k, core) for core in range(2)]) for k in range(group)])
        lines = nn_dot(lines, sort_ref[...]).astype(BF16)
        fields = []
        for k in range(0, group, 2):
            pair = [lines[at * z.lines : (at + 1) * z.lines] for at in (k, k + 1)]
            fields.append(
                stacked([side_by_side([side[:, b : b + n] for side in pair]) for b in range(0, 4 * n, n)] + [ones])
            )
        firsts = [relu(nn_dot(k1_ref[...], field)) for field in fields]
        fields = []
        for first in firsts:
            even, odd = first[: z.m1], first[z.m1 :]
            moves = blocks([even[:, :n], even[:, n:]], [odd[:, :n], odd[:, n:]], lanes1)[2:]
            fields.append(stacked([first] + moves))
        seconds = [relu(nn_dot(k2_ref[...], field)) for field in fields]
        for k, second in enumerate(seconds):
            reduced = relu(nn_dot(k3_ref[...], stacked([second, ones])))
            coarse[base + 2 * k + 1] = reduced[:, :n]
            coarse[base + 2 * k + 2] = reduced[:, n:]

    def trailing(base):
        planes = list(range(-1, group + 1)) if groups > 1 else list(range(group))
        totals = [None] * group
        for q in range(0, len(planes), 2):
            pair = planes[q : q + 2]
            fields = []
            for k in pair:
                plane = coarse[base + k + 1]
                fields.append(stacked([moved(plane, 1, lanes3), plane, moved(plane, -1, lanes3), ones[:, :n]]))
            terms = nn_dot(k4_ref[...], side_by_side(fields))
            for side, k in enumerate(pair):
                for i in range(3):
                    to = k + 1 - i
                    if 0 <= to < group:
                        term = terms[i * z.m4 : (i + 1) * z.m4, side * n : (side + 1) * n]
                        totals[to] = term if totals[to] is None else totals[to] + term
        for k in range(group):
            out_ref[base + k] = relu(totals[k])

    if groups == 1:
        leading(0)
        trailing(0)
    else:
        pl.loop(0, groups)(lambda g: leading(g * group))
        pl.loop(0, groups)(lambda g: trailing(g * group))


def shards(
    volume, first_weight, first_offset, second_weight, second_offset,
    reduce_conv_weight, reduce_conv_bias, deep_weight, deep_offset,
):
    vols, members = lax.axis_size("vol"), lax.axis_size("zs")
    z = Sizes(volume, first_weight, reduce_conv_weight, vols, members)
    slices = volume.shape[0]
    vmem = pl.BlockSpec(memory_space=pltpu.VMEM)
    like = jax.ShapeDtypeStruct
    chips = vols // 2
    other = lax.ppermute(volume, "vol", [(v, v ^ 1) for v in range(vols)])
    own = pl.pallas_call(
        functools.partial(load_kernel, z),
        out_shape=like((slices, z.rows, z.half), F32),
        in_specs=[vmem],
        out_specs=vmem,
        compiler_params=pltpu.CompilerParams(vmem_limit_bytes=16 * 1024 * 1024),
        cost_estimate=pl.CostEstimate(flops=5_000_000, bytes_accessed=100_000, transcendentals=0),
        name="load",
    )(volume)
    packed = pl.pallas_call(
        functools.partial(pack_kernel, z, chips, members),
        out_shape=like((vols * members * slices, 4, z.pieces * z.half), BF16),
        in_specs=[vmem] * 2,
        out_specs=vmem,
        compiler_params=pltpu.CompilerParams(vmem_limit_bytes=16 * 1024 * 1024),
        name="pack",
    )(own, other)
    packed, *parameters = lax.optimization_barrier((
        packed, first_weight, first_offset, second_weight, second_offset,
        reduce_conv_weight, reduce_conv_bias, deep_weight, deep_offset,
    ))
    got = lax.all_to_all(packed, ("vol", "zs"), split_axis=0, concat_axis=0, tiled=True)
    got = got.reshape(chips, 2, z.depth, 4, z.pieces * z.half)
    prepared = pl.pallas_call(
        functools.partial(prepare_kernel, z, members),
        out_shape=(
            like((z.cols, 4 * z.half), BF16),
            like((2 * z.m1, 4 * z.lines + TILE), BF16),
            like((2 * z.m2, 4 * z.m1), BF16),
            like((z.m3, 2 * z.m2 + TILE), BF16),
            like((3 * z.m4, 3 * z.m3 + TILE), BF16),
        ),
        in_specs=[vmem] * 8,
        out_specs=(vmem,) * 5,
        compiler_params=pltpu.CompilerParams(vmem_limit_bytes=16 * 1024 * 1024),
        cost_estimate=pl.CostEstimate(flops=50_000_000, bytes_accessed=1_000_000, transcendentals=0),
        name="prepare",
    )(
        *(value[None] if value.ndim == 1 else value for value in parameters)
    )
    affinity = pl.pallas_call(
        functools.partial(main_kernel, z, chips),
        out_shape=like((z.depth, z.m4, z.half), BF16),
        in_specs=[vmem] * 6,
        out_specs=vmem,
        scratch_shapes=[
            pltpu.VMEM((z.depth + 2, z.m3, z.half), BF16),
        ],
        compiler_params=pltpu.CompilerParams(vmem_limit_bytes=32 * 1024 * 1024),
        cost_estimate=pl.CostEstimate(flops=2_000_000_000, bytes_accessed=2_000_000, transcendentals=0),
        name="encode",
    )(got, *prepared)
    return affinity.reshape(z.depth, z.deep, z.strip, z.half)


def solution(mesh):
    return jax.shard_map(
        shards,
        mesh=mesh,
        in_specs=(P("zs", "vol", None), P(), P(), P(), P(), P(), P(), P(), P()),
        out_specs=P(None, None, ("vol", "zs"), None),
        check_vma=False,
    )
```

```python
import functools

import jax
import jax.numpy as jnp
from jax import lax
from jax.experimental import pallas as pl
from jax.experimental.pallas import tpu as pltpu
from jax.sharding import PartitionSpec as P

TILE = 16
SHIFTS = ((1, 2, 0, None), (0, 1, None, 2))
F32 = jnp.float32
BF16 = jnp.bfloat16


def iota(shape, dim):
    return lax.broadcasted_iota(jnp.int32, shape, dim)


def ceil_to(value, step):
    return -(-value // step) * step


def div(value, by):
    if by & (by - 1) == 0:
        return lax.shift_right_logical(value, by.bit_length() - 1)
    return lax.shift_right_logical(value * (-(-65536 // by)), 16)


def one_hot(condition):
    return jnp.where(condition, 1.0, 0.0).astype(BF16)


def nt_dot(lhs, rhs):
    return lax.dot_general(lhs, rhs, (((1,), (1,)), ((), ())), preferred_element_type=F32)


def nn_dot(lhs, rhs):
    return jnp.dot(lhs, rhs, preferred_element_type=F32)


class Sizes:
    def __init__(self, volume, first_weight, reduce_conv_weight, vols, members):
        self.depth = volume.shape[0] * members
        self.cols = volume.shape[2]
        self.half = self.cols // 2
        self.fine_rows = volume.shape[1] * vols
        self.rows = volume.shape[1]
        self.strip = volume.shape[1] // 2 // members
        self.chan = first_weight.shape[1]
        self.deep = reduce_conv_weight.shape[2]
        self.coarse_rows = self.strip + 2
        self.second_rows = 2 * self.coarse_rows
        self.first_rows = self.second_rows + 2
        self.window = self.first_rows + 2
        self.pieces = self.window // 4
        self.lines = ceil_to(self.window, TILE)
        self.ones1 = self.first_rows * self.chan
        self.m1 = ceil_to(self.ones1 + 3, TILE)
        self.m2 = self.second_rows * self.chan
        self.m3 = self.coarse_rows * self.deep
        self.m4 = self.strip * self.deep

    def base(self, member):
        return 2 * self.strip * member - 4


def sort_kernel(z, own_ref, sort_ref, sorted_ref):
    core = lax.rem(lax.axis_index("vol"), 2)
    shape = (z.cols, z.half)
    sort = one_hot(iota(shape, 0) == 2 * iota(shape, 1) + core)
    sort_ref[...] = sort
    for s in range(own_ref.shape[0]):
        sorted_ref[s] = nn_dot(own_ref[s], sort)


def pack_kernel(z, chips, members, own_ref, sort_ref, other_ref, packed_ref):
    vol = lax.axis_index("vol")
    chip = lax.div(vol, 2)
    first_core = vol - 2 * chip == 0
    packed_ref[...] = jnp.zeros(packed_ref.shape, BF16)
    slices = own_ref.shape[0]
    empty = jnp.zeros((4, z.half), BF16)
    for s in range(slices):
        own, other = own_ref[s], nn_dot(other_ref[s], sort_ref[...])
        lines = stacked([jnp.where(first_core, own, other), jnp.where(first_core, other, own)])
        pieces = [lines[row : row + 4].astype(BF16) for row in range(0, 2 * z.rows, 4)]

        def put(to, first):
            for piece in range(z.pieces):
                at = first // 4 + piece
                value = pieces[at] if 0 <= at < len(pieces) else empty
                packed_ref[(to * slices + s) * z.pieces + piece] = value

        for core in range(2):
            for member in range(members):
                put((2 * chip + core) * members + member, core * z.rows + z.base(member))

        @pl.when(chip < chips - 1)
        def _():
            put(2 * (chip + 1) * members, 2 * z.rows - 4)

        @pl.when(chip > 0)
        def _():
            put(2 * chip * members - 1, 4 - z.window)


def prepare_kernel(
    z, members, w1_ref, b1_ref, w2_ref, b2_ref, w3_ref, b3_ref, w4_ref, b4_ref,
    k1_ref, k2_ref, k3_ref, k4_ref,
):
    member = lax.axis_index("zs")
    start = (lax.axis_index("vol") * members + member) * (2 * z.strip)
    def spread(rows, offsets, period, stretch):
        row = div(iota((rows, period), 0), stretch)
        at = row - div(row, period) * period
        picked = jnp.where(at == iota((rows, period), 1), offsets, 0.0)
        return jnp.sum(picked, axis=1, keepdims=True)

    def bias_terms(column, at):
        high = column.astype(BF16).astype(F32)
        middle = (column - high).astype(BF16).astype(F32)
        low = column - high - middle
        return jnp.where(at == 0, high, jnp.where(at == 1, middle, jnp.where(at == 2, low, 0.0)))

    row = iota((z.m1, z.chan), 0)
    pick = one_hot(row - div(row, z.chan) * z.chan == iota((z.m1, z.chan), 1))
    taps = nt_dot(pick, w1_ref[...]).astype(BF16)
    shape = (z.m1, 4 * z.lines)
    x = div(iota(shape, 0), z.chan)
    col = iota(shape, 1)
    line = col - div(col, z.lines) * z.lines
    inside = (start - 3 + x >= 0) & (start - 3 + x < z.fine_rows) & (x < z.first_rows)
    block = div(iota((9, 4 * z.lines), 1), z.lines)
    narrow = (z.m1, TILE)
    row, col = iota(narrow, 0), iota(narrow, 1)
    narrow_x = div(row, z.chan)
    narrow_inside = (start - 3 + narrow_x >= 0) & (start - 3 + narrow_x < z.fine_rows)
    bias = jnp.where(narrow_inside, bias_terms(spread(z.m1, b1_ref[...], z.chan, 1), col), 0.0)
    ones = jnp.where((row < z.ones1 + 3) & (col == 0), 1.0, 0.0)
    bias = jnp.where(row < z.ones1, bias, ones).astype(BF16)
    for parity, shifts in enumerate(SHIFTS):
        shift = jnp.full(block.shape, 9, jnp.int32)
        for number, value in enumerate(shifts):
            if value is not None:
                shift = jnp.where(block == number, value, shift)
        total = jnp.zeros(shape, F32)
        for i in range(3):
            level = nn_dot(taps, one_hot(iota(block.shape, 0) == 3 * i + shift))
            total += jnp.where(inside & (line == x + i), level, 0.0)
        k1_ref[parity * z.m1 : (parity + 1) * z.m1, : 4 * z.lines] = total.astype(BF16)
        k1_ref[parity * z.m1 : (parity + 1) * z.m1, 4 * z.lines :] = bias

    row = iota((z.m2, z.chan), 0)
    pick = one_hot(row - div(row, z.chan) * z.chan == iota((z.m2, z.chan), 1))
    col = iota((z.chan, z.m1), 1)
    widen = one_hot(col - div(col, z.chan) * z.chan == iota((z.chan, z.m1), 0))
    shape = (z.m2, z.m1)
    lag = div(iota(shape, 1), z.chan) - div(iota(shape, 0), z.chan)
    bias = bias_terms(spread(z.m2, b2_ref[...], z.chan, 1), iota(shape, 1) - z.ones1)
    for s in range(3):
        total = bias if s == 1 else jnp.zeros(shape, F32)
        for i in range(3):
            level = nn_dot(nt_dot(pick, w2_ref[3 * i + s]).astype(BF16), widen)
            total += jnp.where(lag == i, level, 0.0)
        total = total.astype(BF16)
        for parity, shifts in enumerate(SHIFTS):
            at = shifts.index(s)
            k2_ref[parity * z.m2 : (parity + 1) * z.m2, at * z.m1 : (at + 1) * z.m1] = total
    for parity, shifts in enumerate(SHIFTS):
        at = shifts.index(None)
        k2_ref[parity * z.m2 : (parity + 1) * z.m2, at * z.m1 : (at + 1) * z.m1] = jnp.zeros(shape, BF16)

    row = iota((z.m3, z.deep), 0)
    u = div(row, z.deep)
    pick = one_hot(row - u * z.deep == iota((z.m3, z.deep), 1))
    col = iota((z.chan, z.m2), 1)
    widen = one_hot(col - div(col, z.chan) * z.chan == iota((z.chan, z.m2), 0))
    shape = (z.m3, z.m2)
    u = div(iota(shape, 0), z.deep)
    lag = div(iota(shape, 1), z.chan) - 2 * u
    inside = (start + 2 * u >= 2) & (start + 2 * u < z.fine_rows + 2)
    for b in range(2):
        total = jnp.zeros(shape, F32)
        for a in range(2):
            level = nn_dot(nt_dot(pick, w3_ref[2 * a + b]).astype(BF16), widen)
            total += jnp.where(inside & (lag == a), level, 0.0)
        k3_ref[:, b * z.m2 : (b + 1) * z.m2] = total.astype(BF16)
    shape = (z.m3, TILE)
    u = div(iota(shape, 0), z.deep)
    inside = (start + 2 * u >= 2) & (start + 2 * u < z.fine_rows + 2)
    bias = bias_terms(spread(z.m3, b3_ref[...], z.deep, 1), iota(shape, 1))
    k3_ref[:, 2 * z.m2 :] = jnp.where(inside, bias, 0.0).astype(BF16)

    row = iota((z.m4, z.deep), 0)
    pick = one_hot(div(row, z.strip) == iota((z.m4, z.deep), 1))
    col = iota((z.deep, z.m3), 1)
    widen = one_hot(col - div(col, z.deep) * z.deep == iota((z.deep, z.m3), 0))
    shape = (z.m4, z.m3)
    row = iota(shape, 0)
    lag = div(iota(shape, 1), z.deep) - (row - div(row, z.strip) * z.strip)
    for i in range(3):
        for s in range(3):
            total = jnp.zeros(shape, F32)
            for j in range(3):
                level = nn_dot(nt_dot(pick, w4_ref[9 * i + 3 * j + s]).astype(BF16), widen)
                total += jnp.where(lag == j, level, 0.0)
            k4_ref[i * z.m4 : (i + 1) * z.m4, s * z.m3 : (s + 1) * z.m3] = total.astype(BF16)
    shape = (z.m4, TILE)
    bias = bias_terms(spread(z.m4, b4_ref[...], z.deep, z.strip), iota(shape, 1))
    for i in range(3):
        terms = bias if i == 1 else jnp.zeros(shape, F32)
        k4_ref[i * z.m4 : (i + 1) * z.m4, 3 * z.m3 :] = terms.astype(BF16)


def relu(value):
    return jnp.maximum(value.astype(BF16), 0)


def side_by_side(values):
    return jnp.concatenate(values, axis=1)


def stacked(values):
    return jnp.concatenate(values, axis=0)


def moved(value, by, lanes):
    width = value.shape[1]
    turned = pltpu.roll(value, by % width, axis=1)
    edge = 0 if by == 1 else width - 1
    return jnp.where(lanes == edge, jnp.zeros_like(turned), turned)


def main_kernel(
    z, chips, got_ref, k1_ref, k2_ref, k3_ref, k4_ref, out_ref, coarse, result, sems,
):
    chip = lax.div(lax.axis_index("vol"), 2)
    sources = [chip]
    if chips > 1:
        sources.append(lax.rem(chip + 1, chips))
    if chips > 2:
        sources.append(lax.rem(chip + chips - 1, chips))
    group = min(z.depth, 8)
    groups = z.depth // group
    n = z.half
    ones = jnp.ones((TILE, z.cols), BF16)
    blanks = [jnp.zeros((z.lines - z.window, n), F32)] if z.lines > z.window else []
    lanes0 = iota((z.lines, n), 1)
    lanes1 = iota((z.m1, n), 1)
    lanes3 = iota((z.m3, n), 1)
    if groups > 1:
        coarse[0] = jnp.zeros((z.m3, n), BF16)
        coarse[z.depth + 1] = jnp.zeros((z.m3, n), BF16)

    def blocks(evens, odds, lanes):
        odds_right = [moved(odd, 1, lanes) for odd in odds]
        evens_left = [moved(even, -1, lanes) for even in evens]
        return [side_by_side(pair) for pair in (evens, odds, odds_right, evens_left)]

    def lines_of(k, core):
        pieces = []
        for piece in range(z.pieces):
            at = k * z.pieces + piece
            pieces.append(sum(got_ref[source, core, at].astype(F32) for source in sources))
        return stacked(pieces + blanks)

    def leading(base):
        fields = []
        for k in range(0, group, 2):
            evens, odds = ([lines_of(base + k, core), lines_of(base + k + 1, core)] for core in range(2))
            fields.append(stacked([stacked(blocks(evens, odds, lanes0)).astype(BF16), ones]))
        firsts = [relu(nn_dot(k1_ref[...], field)) for field in fields]
        fields = []
        for first in firsts:
            even, odd = first[: z.m1], first[z.m1 :]
            moves = blocks([even[:, :n], even[:, n:]], [odd[:, :n], odd[:, n:]], lanes1)[2:]
            fields.append(stacked([first] + moves))
        seconds = [relu(nn_dot(k2_ref[...], field)) for field in fields]
        for k, second in enumerate(seconds):
            reduced = relu(nn_dot(k3_ref[...], stacked([second, ones])))
            coarse[base + 2 * k + 1] = reduced[:, :n]
            coarse[base + 2 * k + 2] = reduced[:, n:]

    def trailing(base):
        planes = list(range(-1, group + 1)) if groups > 1 else list(range(group))
        totals = {}
        half = max(group // 2, 1)
        copies = [
            pltpu.make_async_copy(result.at[pl.ds(at, half)], out_ref.at[pl.ds(base + at, half)], sems.at[number])
            for number, at in enumerate(range(0, group, half))
        ]
        written = 0
        for q in range(0, len(planes), 2):
            pair = planes[q : q + 2]
            fields = []
            for k in pair:
                plane = coarse[base + k + 1]
                fields.append(stacked([moved(plane, 1, lanes3), plane, moved(plane, -1, lanes3), ones[:, :n]]))
            terms = nn_dot(k4_ref[...], side_by_side(fields))
            for side, k in enumerate(pair):
                for i in range(3):
                    to = k + 1 - i
                    term = terms[i * z.m4 : (i + 1) * z.m4, side * n : (side + 1) * n]
                    totals[to] = totals[to] + term if to in totals else term
            done = group if pair[-1] == planes[-1] else pair[-1]
            while written < done:
                result[written] = relu(totals[written])
                written += 1
                if written % half == 0:
                    copies[written // half - 1].start()
        for copy in copies:
            copy.wait()

    if groups == 1:
        leading(0)
        trailing(0)
    else:
        pl.loop(0, groups)(lambda g: leading(g * group))
        pl.loop(0, groups)(lambda g: trailing(g * group))


def shards(
    volume, first_weight, first_offset, second_weight, second_offset,
    reduce_conv_weight, reduce_conv_bias, deep_weight, deep_offset,
):
    vols, members = lax.axis_size("vol"), lax.axis_size("zs")
    z = Sizes(volume, first_weight, reduce_conv_weight, vols, members)
    slices = volume.shape[0]
    vmem = pl.BlockSpec(memory_space=pltpu.VMEM)
    like = jax.ShapeDtypeStruct
    chips = vols // 2
    other = lax.ppermute(volume, "vol", [(v, v ^ 1) for v in range(vols)])
    sort, own = pl.pallas_call(
        functools.partial(sort_kernel, z),
        out_shape=(like((z.cols, z.half), BF16), like((slices, z.rows, z.half), F32)),
        in_specs=[vmem],
        out_specs=(vmem,) * 2,
        compiler_params=pltpu.CompilerParams(vmem_limit_bytes=16 * 1024 * 1024),
        cost_estimate=pl.CostEstimate(flops=5_000_000, bytes_accessed=100_000, transcendentals=0),
        name="sort",
    )(volume)
    packed = pl.pallas_call(
        functools.partial(pack_kernel, z, chips, members),
        out_shape=like((vols * members * slices * z.pieces, 4, z.half), BF16),
        in_specs=[vmem] * 3,
        out_specs=vmem,
        compiler_params=pltpu.CompilerParams(vmem_limit_bytes=16 * 1024 * 1024),
        name="pack",
    )(own, sort, other)
    packed, *parameters = lax.optimization_barrier((
        packed, first_weight, first_offset, second_weight, second_offset,
        reduce_conv_weight, reduce_conv_bias, deep_weight, deep_offset,
    ))
    got = lax.all_to_all(packed, ("vol", "zs"), split_axis=0, concat_axis=0, tiled=True)
    got = got.reshape(chips, 2, z.depth * z.pieces, 4, z.half)
    prepared = pl.pallas_call(
        functools.partial(prepare_kernel, z, members),
        out_shape=(
            like((2 * z.m1, 4 * z.lines + TILE), BF16),
            like((2 * z.m2, 4 * z.m1), BF16),
            like((z.m3, 2 * z.m2 + TILE), BF16),
            like((3 * z.m4, 3 * z.m3 + TILE), BF16),
        ),
        in_specs=[vmem] * 8,
        out_specs=(vmem,) * 4,
        compiler_params=pltpu.CompilerParams(vmem_limit_bytes=16 * 1024 * 1024),
        cost_estimate=pl.CostEstimate(flops=50_000_000, bytes_accessed=1_000_000, transcendentals=0),
        name="prepare",
    )(
        *(value[None] if value.ndim == 1 else value for value in parameters)
    )
    affinity = pl.pallas_call(
        functools.partial(main_kernel, z, chips),
        out_shape=like((z.depth, z.m4, z.half), BF16),
        in_specs=[vmem] * 5,
        out_specs=pl.BlockSpec(memory_space=pl.ANY),
        scratch_shapes=[
            pltpu.VMEM((z.depth + 2, z.m3, z.half), BF16),
            pltpu.VMEM((min(z.depth, 8), z.m4, z.half), BF16),
            pltpu.SemaphoreType.DMA((2,)),
        ],
        compiler_params=pltpu.CompilerParams(vmem_limit_bytes=32 * 1024 * 1024),
        cost_estimate=pl.CostEstimate(flops=2_000_000_000, bytes_accessed=2_000_000, transcendentals=0),
        name="encode",
    )(got, *prepared)
    return affinity.reshape(z.depth, z.deep, z.strip, z.half)


def solution(mesh):
    return jax.shard_map(
        shards,
        mesh=mesh,
        in_specs=(P("zs", "vol", None), P(), P(), P(), P(), P(), P(), P(), P()),
        out_specs=P(None, None, ("vol", "zs"), None),
        check_vma=False,
    )
```

```python
import functools

import jax
import jax.numpy as jnp
from jax import lax
from jax.experimental import pallas as pl
from jax.experimental.pallas import tpu as pltpu
from jax.sharding import PartitionSpec as P

TILE = 16
SHIFTS = ((1, 2, 0, None), (0, 1, None, 2))
F32 = jnp.float32
BF16 = jnp.bfloat16


def iota(shape, dim):
    return lax.broadcasted_iota(jnp.int32, shape, dim)


def ceil_to(value, step):
    return -(-value // step) * step


def div(value, by):
    if by & (by - 1) == 0:
        return lax.shift_right_logical(value, by.bit_length() - 1)
    return lax.shift_right_logical(value * (-(-65536 // by)), 16)


def one_hot(condition):
    return jnp.where(condition, 1.0, 0.0).astype(BF16)


def nt_dot(lhs, rhs):
    return lax.dot_general(lhs, rhs, (((1,), (1,)), ((), ())), preferred_element_type=F32)


def nn_dot(lhs, rhs):
    return jnp.dot(lhs, rhs, preferred_element_type=F32)


class Sizes:
    def __init__(self, volume, first_weight, reduce_conv_weight, vols, members):
        self.depth = volume.shape[0] * members
        self.cols = volume.shape[2]
        self.half = self.cols // 2
        self.fine_rows = volume.shape[1] * vols
        self.rows = volume.shape[1]
        self.strip = volume.shape[1] // 2 // members
        self.chan = first_weight.shape[1]
        self.deep = reduce_conv_weight.shape[2]
        self.coarse_rows = self.strip + 2
        self.second_rows = 2 * self.coarse_rows
        self.first_rows = self.second_rows + 2
        self.window = self.first_rows + 2
        self.pieces = self.window // 4
        self.lines = ceil_to(self.window, TILE)
        self.ones1 = self.first_rows * self.chan
        self.m1 = ceil_to(self.ones1 + 3, TILE)
        self.m2 = self.second_rows * self.chan
        self.m3 = self.coarse_rows * self.deep
        self.m4 = self.strip * self.deep

    def base(self, member):
        return 2 * self.strip * member - 4


def sort_kernel(z, own_ref, sort_ref, sorted_ref):
    core = lax.rem(lax.axis_index("vol"), 2)
    shape = (z.cols, z.half)
    sort = one_hot(iota(shape, 0) == 2 * iota(shape, 1) + core)
    sort_ref[...] = sort
    for s in range(own_ref.shape[0]):
        sorted_ref[s] = nn_dot(own_ref[s], sort)


def pack_kernel(z, chips, members, own_ref, sort_ref, other_ref, packed_ref):
    vol = lax.axis_index("vol")
    chip = lax.div(vol, 2)
    first_core = vol - 2 * chip == 0
    packed_ref[...] = jnp.zeros(packed_ref.shape, BF16)
    slices = own_ref.shape[0]
    empty = jnp.zeros((4, z.half), BF16)
    for s in range(slices):
        own, other = own_ref[s], nn_dot(other_ref[s], sort_ref[...])
        lines = stacked([jnp.where(first_core, own, other), jnp.where(first_core, other, own)])
        pieces = [lines[row : row + 4].astype(BF16) for row in range(0, 2 * z.rows, 4)]

        def put(to, first):
            for piece in range(z.pieces):
                at = first // 4 + piece
                value = pieces[at] if 0 <= at < len(pieces) else empty
                packed_ref[to * slices + s, :, piece * z.half : (piece + 1) * z.half] = value

        for core in range(2):
            for member in range(members):
                put((2 * chip + core) * members + member, core * z.rows + z.base(member))

        @pl.when(chip < chips - 1)
        def _():
            put(2 * (chip + 1) * members, 2 * z.rows - 4)

        @pl.when(chip > 0)
        def _():
            put(2 * chip * members - 1, 4 - z.window)


def prepare_kernel(
    z, members, w1_ref, b1_ref, w2_ref, b2_ref, w3_ref, b3_ref, w4_ref, b4_ref,
    k1_ref, k2_ref, k3_ref, k4_ref,
):
    member = lax.axis_index("zs")
    start = (lax.axis_index("vol") * members + member) * (2 * z.strip)
    def spread(rows, offsets, period, stretch):
        row = div(iota((rows, period), 0), stretch)
        at = row - div(row, period) * period
        picked = jnp.where(at == iota((rows, period), 1), offsets, 0.0)
        return jnp.sum(picked, axis=1, keepdims=True)

    def bias_terms(column, at):
        high = column.astype(BF16).astype(F32)
        middle = (column - high).astype(BF16).astype(F32)
        low = column - high - middle
        return jnp.where(at == 0, high, jnp.where(at == 1, middle, jnp.where(at == 2, low, 0.0)))

    row = iota((z.m1, z.chan), 0)
    pick = one_hot(row - div(row, z.chan) * z.chan == iota((z.m1, z.chan), 1))
    taps = nt_dot(pick, w1_ref[...]).astype(BF16)
    shape = (z.m1, 4 * z.lines)
    x = div(iota(shape, 0), z.chan)
    col = iota(shape, 1)
    line = col - div(col, z.lines) * z.lines
    inside = (start - 3 + x >= 0) & (start - 3 + x < z.fine_rows) & (x < z.first_rows)
    block = div(iota((9, 4 * z.lines), 1), z.lines)
    narrow = (z.m1, TILE)
    row, col = iota(narrow, 0), iota(narrow, 1)
    narrow_x = div(row, z.chan)
    narrow_inside = (start - 3 + narrow_x >= 0) & (start - 3 + narrow_x < z.fine_rows)
    bias = jnp.where(narrow_inside, bias_terms(spread(z.m1, b1_ref[...], z.chan, 1), col), 0.0)
    ones = jnp.where((row < z.ones1 + 3) & (col == 0), 1.0, 0.0)
    bias = jnp.where(row < z.ones1, bias, ones).astype(BF16)
    for parity, shifts in enumerate(SHIFTS):
        shift = jnp.full(block.shape, 9, jnp.int32)
        for number, value in enumerate(shifts):
            if value is not None:
                shift = jnp.where(block == number, value, shift)
        total = jnp.zeros(shape, F32)
        for i in range(3):
            level = nn_dot(taps, one_hot(iota(block.shape, 0) == 3 * i + shift))
            total += jnp.where(inside & (line == x + i), level, 0.0)
        k1_ref[parity * z.m1 : (parity + 1) * z.m1, : 4 * z.lines] = total.astype(BF16)
        k1_ref[parity * z.m1 : (parity + 1) * z.m1, 4 * z.lines :] = bias

    row = iota((z.m2, z.chan), 0)
    pick = one_hot(row - div(row, z.chan) * z.chan == iota((z.m2, z.chan), 1))
    col = iota((z.chan, z.m1), 1)
    widen = one_hot(col - div(col, z.chan) * z.chan == iota((z.chan, z.m1), 0))
    shape = (z.m2, z.m1)
    lag = div(iota(shape, 1), z.chan) - div(iota(shape, 0), z.chan)
    bias = bias_terms(spread(z.m2, b2_ref[...], z.chan, 1), iota(shape, 1) - z.ones1)
    for s in range(3):
        total = bias if s == 1 else jnp.zeros(shape, F32)
        for i in range(3):
            level = nn_dot(nt_dot(pick, w2_ref[3 * i + s]).astype(BF16), widen)
            total += jnp.where(lag == i, level, 0.0)
        total = total.astype(BF16)
        for parity, shifts in enumerate(SHIFTS):
            at = shifts.index(s)
            k2_ref[parity * z.m2 : (parity + 1) * z.m2, at * z.m1 : (at + 1) * z.m1] = total
    for parity, shifts in enumerate(SHIFTS):
        at = shifts.index(None)
        k2_ref[parity * z.m2 : (parity + 1) * z.m2, at * z.m1 : (at + 1) * z.m1] = jnp.zeros(shape, BF16)

    row = iota((z.m3, z.deep), 0)
    u = div(row, z.deep)
    pick = one_hot(row - u * z.deep == iota((z.m3, z.deep), 1))
    col = iota((z.chan, z.m2), 1)
    widen = one_hot(col - div(col, z.chan) * z.chan == iota((z.chan, z.m2), 0))
    shape = (z.m3, z.m2)
    u = div(iota(shape, 0), z.deep)
    lag = div(iota(shape, 1), z.chan) - 2 * u
    inside = (start + 2 * u >= 2) & (start + 2 * u < z.fine_rows + 2)
    for b in range(2):
        total = jnp.zeros(shape, F32)
        for a in range(2):
            level = nn_dot(nt_dot(pick, w3_ref[2 * a + b]).astype(BF16), widen)
            total += jnp.where(inside & (lag == a), level, 0.0)
        k3_ref[:, b * z.m2 : (b + 1) * z.m2] = total.astype(BF16)
    shape = (z.m3, TILE)
    u = div(iota(shape, 0), z.deep)
    inside = (start + 2 * u >= 2) & (start + 2 * u < z.fine_rows + 2)
    bias = bias_terms(spread(z.m3, b3_ref[...], z.deep, 1), iota(shape, 1))
    k3_ref[:, 2 * z.m2 :] = jnp.where(inside, bias, 0.0).astype(BF16)

    row = iota((z.m4, z.deep), 0)
    pick = one_hot(div(row, z.strip) == iota((z.m4, z.deep), 1))
    col = iota((z.deep, z.m3), 1)
    widen = one_hot(col - div(col, z.deep) * z.deep == iota((z.deep, z.m3), 0))
    shape = (z.m4, z.m3)
    row = iota(shape, 0)
    lag = div(iota(shape, 1), z.deep) - (row - div(row, z.strip) * z.strip)
    for i in range(3):
        for s in range(3):
            total = jnp.zeros(shape, F32)
            for j in range(3):
                level = nn_dot(nt_dot(pick, w4_ref[9 * i + 3 * j + s]).astype(BF16), widen)
                total += jnp.where(lag == j, level, 0.0)
            k4_ref[i * z.m4 : (i + 1) * z.m4, s * z.m3 : (s + 1) * z.m3] = total.astype(BF16)
    shape = (z.m4, TILE)
    bias = bias_terms(spread(z.m4, b4_ref[...], z.deep, z.strip), iota(shape, 1))
    for i in range(3):
        terms = bias if i == 1 else jnp.zeros(shape, F32)
        k4_ref[i * z.m4 : (i + 1) * z.m4, 3 * z.m3 :] = terms.astype(BF16)


def relu(value):
    return jnp.maximum(value.astype(BF16), 0)


def side_by_side(values):
    return jnp.concatenate(values, axis=1)


def stacked(values):
    return jnp.concatenate(values, axis=0)


def moved(value, by, lanes):
    width = value.shape[1]
    turned = pltpu.roll(value, by % width, axis=1)
    edge = 0 if by == 1 else width - 1
    return jnp.where(lanes == edge, jnp.zeros_like(turned), turned)


def main_kernel(
    z, chips, got_ref, k1_ref, k2_ref, k3_ref, k4_ref, out_ref, coarse, result, sems,
):
    chip = lax.div(lax.axis_index("vol"), 2)
    sources = [chip]
    if chips > 1:
        sources.append(lax.rem(chip + 1, chips))
    if chips > 2:
        sources.append(lax.rem(chip + chips - 1, chips))
    group = min(z.depth, 8)
    groups = z.depth // group
    n = z.half
    ones = jnp.ones((TILE, z.cols), BF16)
    blanks = [jnp.zeros((z.lines - z.window, n), F32)] if z.lines > z.window else []
    lanes0 = iota((z.lines, n), 1)
    lanes1 = iota((z.m1, n), 1)
    lanes3 = iota((z.m3, n), 1)
    if groups > 1:
        coarse[0] = jnp.zeros((z.m3, n), BF16)
        coarse[z.depth + 1] = jnp.zeros((z.m3, n), BF16)

    def blocks(evens, odds, lanes):
        odds_right = [moved(odd, 1, lanes) for odd in odds]
        evens_left = [moved(even, -1, lanes) for even in evens]
        return [side_by_side(pair) for pair in (evens, odds, odds_right, evens_left)]

    def lines_of(k, core):
        window = sum(got_ref[source, core, k].astype(F32) for source in sources)
        lines = [window[:, piece * n : (piece + 1) * n] for piece in range(z.pieces)]
        return stacked(lines + blanks).astype(BF16)

    def leading(base):
        fields = []
        for k in range(0, group, 2):
            evens, odds = ([lines_of(base + k, core), lines_of(base + k + 1, core)] for core in range(2))
            fields.append(stacked(blocks(evens, odds, lanes0) + [ones]))
        firsts = [relu(nn_dot(k1_ref[...], field)) for field in fields]
        fields = []
        for first in firsts:
            even, odd = first[: z.m1], first[z.m1 :]
            moves = blocks([even[:, :n], even[:, n:]], [odd[:, :n], odd[:, n:]], lanes1)[2:]
            fields.append(stacked([first] + moves))
        seconds = [relu(nn_dot(k2_ref[...], field)) for field in fields]
        for k, second in enumerate(seconds):
            reduced = relu(nn_dot(k3_ref[...], stacked([second, ones])))
            coarse[base + 2 * k + 1] = reduced[:, :n]
            coarse[base + 2 * k + 2] = reduced[:, n:]

    def trailing(base):
        planes = list(range(-1, group + 1)) if groups > 1 else list(range(group))
        totals = {}
        half = max(group // 2, 1)
        copies = [
            pltpu.make_async_copy(result.at[pl.ds(at, half)], out_ref.at[pl.ds(base + at, half)], sems.at[number])
            for number, at in enumerate(range(0, group, half))
        ]
        written = 0
        for q in range(0, len(planes), 2):
            pair = planes[q : q + 2]
            fields = []
            for k in pair:
                plane = coarse[base + k + 1]
                fields.append(stacked([moved(plane, 1, lanes3), plane, moved(plane, -1, lanes3), ones[:, :n]]))
            terms = nn_dot(k4_ref[...], side_by_side(fields))
            for side, k in enumerate(pair):
                for i in range(3):
                    to = k + 1 - i
                    term = terms[i * z.m4 : (i + 1) * z.m4, side * n : (side + 1) * n]
                    totals[to] = totals[to] + term if to in totals else term
            done = group if pair[-1] == planes[-1] else pair[-1]
            while written < done:
                result[written] = relu(totals[written])
                written += 1
                if written % half == 0:
                    copies[written // half - 1].start()
        for copy in copies:
            copy.wait()

    if groups == 1:
        leading(0)
        trailing(0)
    else:
        pl.loop(0, groups)(lambda g: leading(g * group))
        pl.loop(0, groups)(lambda g: trailing(g * group))


def shards(
    volume, first_weight, first_offset, second_weight, second_offset,
    reduce_conv_weight, reduce_conv_bias, deep_weight, deep_offset,
):
    vols, members = lax.axis_size("vol"), lax.axis_size("zs")
    z = Sizes(volume, first_weight, reduce_conv_weight, vols, members)
    slices = volume.shape[0]
    vmem = pl.BlockSpec(memory_space=pltpu.VMEM)
    like = jax.ShapeDtypeStruct
    chips = vols // 2
    other = lax.ppermute(volume, "vol", [(v, v ^ 1) for v in range(vols)])
    sort, own = pl.pallas_call(
        functools.partial(sort_kernel, z),
        out_shape=(like((z.cols, z.half), BF16), like((slices, z.rows, z.half), F32)),
        in_specs=[vmem],
        out_specs=(vmem,) * 2,
        compiler_params=pltpu.CompilerParams(vmem_limit_bytes=16 * 1024 * 1024),
        cost_estimate=pl.CostEstimate(flops=5_000_000, bytes_accessed=100_000, transcendentals=0),
        name="sort",
    )(volume)
    packed = pl.pallas_call(
        functools.partial(pack_kernel, z, chips, members),
        out_shape=like((vols * members * slices, 4, z.pieces * z.half), BF16),
        in_specs=[vmem] * 3,
        out_specs=vmem,
        compiler_params=pltpu.CompilerParams(vmem_limit_bytes=16 * 1024 * 1024),
        name="pack",
    )(own, sort, other)
    packed, *parameters = lax.optimization_barrier((
        packed, first_weight, first_offset, second_weight, second_offset,
        reduce_conv_weight, reduce_conv_bias, deep_weight, deep_offset,
    ))
    got = lax.all_to_all(packed, ("vol", "zs"), split_axis=0, concat_axis=0, tiled=True)
    got = got.reshape(chips, 2, z.depth, 4, z.pieces * z.half)
    prepared = pl.pallas_call(
        functools.partial(prepare_kernel, z, members),
        out_shape=(
            like((2 * z.m1, 4 * z.lines + TILE), BF16),
            like((2 * z.m2, 4 * z.m1), BF16),
            like((z.m3, 2 * z.m2 + TILE), BF16),
            like((3 * z.m4, 3 * z.m3 + TILE), BF16),
        ),
        in_specs=[vmem] * 8,
        out_specs=(vmem,) * 4,
        compiler_params=pltpu.CompilerParams(vmem_limit_bytes=16 * 1024 * 1024),
        cost_estimate=pl.CostEstimate(flops=50_000_000, bytes_accessed=1_000_000, transcendentals=0),
        name="prepare",
    )(
        *(value[None] if value.ndim == 1 else value for value in parameters)
    )
    affinity = pl.pallas_call(
        functools.partial(main_kernel, z, chips),
        out_shape=like((z.depth, z.m4, z.half), BF16),
        in_specs=[vmem] * 5,
        out_specs=pl.BlockSpec(memory_space=pl.ANY),
        scratch_shapes=[
            pltpu.VMEM((z.depth + 2, z.m3, z.half), BF16),
            pltpu.VMEM((min(z.depth, 8), z.m4, z.half), BF16),
            pltpu.SemaphoreType.DMA((2,)),
        ],
        compiler_params=pltpu.CompilerParams(vmem_limit_bytes=32 * 1024 * 1024),
        cost_estimate=pl.CostEstimate(flops=2_000_000_000, bytes_accessed=2_000_000, transcendentals=0),
        name="encode",
    )(got, *prepared)
    return affinity.reshape(z.depth, z.deep, z.strip, z.half)


def solution(mesh):
    return jax.shard_map(
        shards,
        mesh=mesh,
        in_specs=(P("zs", "vol", None), P(), P(), P(), P(), P(), P(), P(), P()),
        out_specs=P(None, None, ("vol", "zs"), None),
        check_vma=False,
    )
```
